32 devices in a mesh: grp: 1, pool: 1, ep: 8 (over z, y), tp: 4 (over x, core).
Axes of the slice: x: 2, y: 2, z: 4, core: 2. Of those that a mesh axis runs over, the one named last changes fastest.
Arguments:
- queries: bfloat16 [1024, 4096], P(('grp', 'ep'), ('pool', 'tp')), may hold values from -6 to 6
- keys_values: bfloat16 [1024, 1024], P(('grp', 'ep'), 'pool'), may hold values from -6 to 6
- residual: bfloat16 [1024, 2048], P(('grp', 'ep', 'tp'), 'pool'), may hold values from -24 to 24
- norm_gain: float32 [2048], P('pool'), may hold values from 0.1 to 1.9
- w_out: bfloat16 [4096, 2048], P(('pool', 'tp')), may hold values from -0.75 to 0.75
- w_gate_up: bfloat16 [32, 2048, 768], P(('ep', 'tp'), 'pool'), may hold values from -0.125 to 0.125
- w_down: bfloat16 [32, 384, 2048], P(('ep', 'tp'), None, 'pool'), may hold values from -0.3125 to 0.3125
- expert_ids: int32 [1024, 8], P(('grp', 'ep', 'tp')), may hold values from 0 to 31, as said below
- mix_weights: float32 [1024, 8], P(('grp', 'ep', 'tp')), may hold values from 0.1 to 1
- clip_lengths: int32 [3], P('grp'), may hold values from 129 to 512, as said below
Outputs:
- layer_out: bfloat16 [1024, 2048], P(('grp', 'ep', 'tp'), 'pool')
The draws below stay inside these ranges and needn't reach their ends.
Inputs may be any that keep to these rules, and one draw needn't show every extreme that they name: `clip_lengths`: 3 clips cover the 1024 tokens; one clip has exactly 512 tokens. `expert_ids`: each row names 8 different experts. Among the 32 rows of one device (aligned blocks of rows) no expert is named more than 16 times, and one expert is named exactly 16 times in every block.
All inputs are finite; a program needn't handle non-finite values.
Results may differ from the reference program's by a relative error of at most 0.018.
Values may be sent and summed in bfloat16 or wider, within the bound.
A program may use at most 64 MiB of HBM per device.

```python
import math
import jax
import jax.numpy as jnp
from jax import lax

D = 2048
QH = 32
KVH = 4
HD = 128
FF = 384
TOP = 8
TOKENS = 1024
CLIP = 512
EXPERTS = 32
GROUP_ROWS = 32
CAP = 16
HEAD_SETS = 4
SET_HEADS = 8
N_EP = 8
N_TP = 4


def draw_queries(key, part):
    drawn = jax.random.normal(jax.random.fold_in(key, 11), (TOKENS, QH * HD), jnp.float32)
    return jnp.clip(1.4 * drawn, -6.0, 6.0).astype(jnp.bfloat16)


def draw_keys_values(key, part):
    drawn = jax.random.normal(jax.random.fold_in(key, 21), (TOKENS, KVH * 2 * HD), jnp.float32)
    return jnp.clip(1.4 * drawn, -6.0, 6.0).astype(jnp.bfloat16)


def draw_residual(key, part):
    columns = jnp.arange(D, dtype=jnp.float32) / D
    rough = jnp.exp(jax.random.uniform(jax.random.fold_in(key, 52), (D,), jnp.float32, -0.3567, 0.3365))
    drawn = jax.random.normal(jax.random.fold_in(key, 51), (TOKENS, D), jnp.float32)
    rise = 3.0 ** (2.0 * columns - 1.0)
    values = jnp.clip(drawn, -4.0, 4.0) * rise[None, :] * rough[None, :]
    return jnp.clip(values, -24.0, 24.0).astype(jnp.bfloat16)


def draw_clip_lengths(key, part):
    count = TOKENS // CLIP
    rest = TOKENS - CLIP
    base = rest // count
    shifts = jax.random.randint(jax.random.fold_in(key, 31), (count,), 0, CLIP // 4)
    others = base + shifts - jnp.roll(shifts, 1)
    others = others.at[0].add(rest - base * count)
    where = jax.random.randint(jax.random.fold_in(key, 32), (), 0, count + 1)
    positions = jnp.arange(count + 1, dtype=jnp.int32)
    source = jnp.where(positions < where, positions, positions - 1)
    picked = others[jnp.clip(source, 0, count - 1)]
    return jnp.where(positions == where, CLIP, picked).astype(jnp.int32)


def permute_experts(one_key):
    return jax.random.permutation(one_key, EXPERTS)


def draw_expert_ids(key, part):
    blocks = TOKENS // GROUP_ROWS
    pairs = EXPERTS // 2
    order_all = jax.random.permutation(jax.random.fold_in(key, 41), EXPERTS).astype(jnp.int32)
    bias = jax.random.randint(jax.random.fold_in(key, 42), (1, pairs), 0, CAP + 1)
    noise = jax.random.randint(jax.random.fold_in(key, 43), (blocks, pairs), -(CAP // 2), CAP // 2 + 1)
    first = jnp.clip(bias + noise, 0, CAP)
    spare = jax.random.randint(jax.random.fold_in(key, 44), (blocks,), 0, CAP + 1)
    share = jax.random.randint(jax.random.fold_in(key, 45), (blocks,), 0, CAP + 1)
    second = CAP - first
    first = first.at[:, 0].set(CAP)
    second = second.at[:, 0].set(spare)
    split = (CAP - spare) * share // CAP
    first = first.at[:, 1].set(split)
    second = second.at[:, 1].set(CAP - spare - split)
    counts = jnp.zeros((blocks, EXPERTS), jnp.int32)
    counts = counts.at[:, order_all[0::2]].set(first).at[:, order_all[1::2]].set(second)
    orders = jax.vmap(permute_experts)(jax.random.split(jax.random.fold_in(key, 46), blocks)).astype(jnp.int32)
    ordered = jnp.take_along_axis(counts, orders, axis=1)
    ends = jnp.cumsum(ordered, axis=1)
    places = jnp.arange(GROUP_ROWS * TOP, dtype=jnp.int32)
    which = jnp.sum((ends[:, None, :] <= places[None, :, None]).astype(jnp.int32), axis=2)
    sequence = jnp.take_along_axis(orders, which, axis=1)
    return sequence.reshape(blocks, TOP, GROUP_ROWS).transpose(0, 2, 1).reshape(TOKENS, TOP).astype(jnp.int32)


def with_spikes(drawn, stream_key, source, target, blocks, factor):
    owner, partner = [(jnp.arange(drawn.shape[dim]) // (drawn.shape[dim] // blocks)).reshape([-1 if axis == dim else 1 for axis in range(drawn.ndim)]) for dim in (source, target)]
    chosen = jax.random.permutation(stream_key, blocks)[partner]
    strong = (owner == chosen) | (owner == (partner + blocks // 2) % blocks)
    return jnp.where(strong, factor * drawn, drawn)


def level_of(own_key, dims, shards, smallest, top_value):
    level = 1.0
    for position, shards_of in shards:
        steps = jax.random.uniform(jax.random.fold_in(jax.random.fold_in(own_key, 6), position), (shards_of,), jnp.float32, smallest / len(shards), top_value / len(shards))
        level = level * jnp.repeat(jnp.exp(steps), dims[position] // shards_of).reshape((-1,) + (1,) * (len(dims) - 1 - position))
    return level


def gaussian(key, dims, deviation, reach, shards=(), kind=jnp.bfloat16):
    level = level_of(key, dims, shards, -0.22, 0.18) if shards else 1.0
    drawn = jax.random.normal(key, dims, jnp.float32) * deviation * level
    return jnp.minimum(jnp.maximum(drawn, -reach), reach).astype(kind)


def gaussian_with(own_key, extent, width, bound, pieces, heavy, held_as=jnp.bfloat16):
    values = width * jax.random.normal(own_key, extent, jnp.float32)
    if pieces:
        values = values * level_of(own_key, extent, pieces, -0.22, 0.18)
    return jnp.clip(with_spikes(values, jax.random.fold_in(own_key, 3), *heavy), -bound, bound).astype(held_as)


def setup_inputs(seed: int = 0, part: int = 0) -> dict:
    splits = jax.random.split(jax.random.key(seed), 11)
    own_keys = jax.random.split(jax.random.fold_in(splits[10], part), 11)
    return {
        "queries": draw_queries(jax.random.fold_in(jax.random.fold_in(splits[10], part), 71), part),
        "keys_values": draw_keys_values(jax.random.fold_in(jax.random.fold_in(splits[10], part), 71), part),
        "residual": draw_residual(jax.random.fold_in(jax.random.fold_in(splits[10], part), 71), part),
        "norm_gain": jnp.clip(1.0 + 0.18 * jax.random.normal(splits[3], (D,), jnp.float32), 0.1, 1.9),
        "w_out": gaussian_with(splits[4], (QH * HD, D), HD ** -0.5, 0.75, ((0, 4),), (0, 1, 4, 2.0)),
        "w_gate_up": gaussian(splits[5], (EXPERTS, D, 2 * FF), D ** -0.5, 0.125, ((0, 32),)),
        "w_down": gaussian(splits[6], (EXPERTS, FF, D), FF ** -0.5, 0.3125, ((0, 32),)),
        "expert_ids": draw_expert_ids(jax.random.fold_in(jax.random.fold_in(splits[10], part), 71), part),
        "mix_weights": jnp.clip(jnp.exp(math.log(1.0) - 2.3025851 * jax.random.uniform(own_keys[8], (TOKENS, TOP), jnp.float32) ** level_of(own_keys[8], (TOKENS, TOP), ((0, 32),), -0.2, 0.2)), 0.1, 1.0),
        "clip_lengths": draw_clip_lengths(jax.random.fold_in(jax.random.fold_in(splits[10], part), 71), part),
    }


def clip_index(clip_lengths, count):
    ends = jnp.cumsum(clip_lengths)
    places = jnp.arange(count, dtype=jnp.int32)
    return lax.optimization_barrier(jnp.sum((places[:, None] >= ends[None, :]).astype(jnp.int32), axis=1))

def attend_head(query, keys, values, clips_of):
    scores = jnp.dot(query.astype(jnp.float32), keys.astype(jnp.float32).T) * HD ** (-0.5)
    same = clips_of[:, None] == clips_of[None, :]
    masked = jnp.where(same, scores, -1e+30)
    top = lax.optimization_barrier(jnp.max(masked, axis=1, keepdims=True))
    weights = jnp.where(same, jnp.exp(masked - top), 0.0)
    denom = lax.optimization_barrier(jnp.sum(weights, axis=1, keepdims=True))
    probs = weights.astype(jnp.bfloat16)
    numer = jnp.dot(probs.astype(jnp.float32), values.astype(jnp.float32))
    return (numer / denom).astype(jnp.bfloat16)

def reference(queries, keys_values, residual, norm_gain, w_out, w_gate_up, w_down, expert_ids, mix_weights, clip_lengths):
    clips_of = clip_index(clip_lengths, TOKENS)
    group = QH // KVH

    def one_head(head):
        query = lax.dynamic_slice_in_dim(queries, head * HD, HD, 1)
        base = head // group * (2 * HD)
        keys = lax.dynamic_slice_in_dim(keys_values, base, HD, 1)
        values = lax.dynamic_slice_in_dim(keys_values, base + HD, HD, 1)
        return attend_head(query, keys, values, clips_of)
    heads = lax.map(one_head, jnp.arange(QH, dtype=jnp.int32))
    head_sets = heads.reshape(HEAD_SETS, SET_HEADS, TOKENS, HD)
    weight_sets = w_out.reshape(HEAD_SETS, SET_HEADS, HD, D)

    def add_set(total, pair):
        part_heads, part_weights = pair
        term = jnp.einsum('htd,hde->te', part_heads.astype(jnp.float32), part_weights.astype(jnp.float32))
        rounded = lax.optimization_barrier(term.astype(jnp.bfloat16))
        return (total + rounded.astype(jnp.float32), None)
    attn_sum, _ = lax.scan(add_set, jnp.zeros((TOKENS, D), jnp.float32), (head_sets, weight_sets))
    hidden_state = residual.astype(jnp.float32) + attn_sum
    mean_square = lax.optimization_barrier(jnp.mean(hidden_state * hidden_state, axis=1))
    normed = (hidden_state * lax.rsqrt(mean_square + 1e-06)[:, None] * norm_gain[None, :]).astype(jnp.bfloat16)
    flat = expert_ids.reshape(-1)
    order = jnp.argsort(flat, stable=True).astype(jnp.int32)
    counts = lax.optimization_barrier(jnp.sum((flat[:, None] == jnp.arange(EXPERTS, dtype=jnp.int32)[None, :]).astype(jnp.int32), axis=0))
    starts = jnp.cumsum(counts) - counts
    most = N_EP * N_TP * CAP
    slots = jnp.arange(most, dtype=jnp.int32)
    assigned = TOKENS * TOP

    def run_expert(carry, expert):
        place = starts[expert] + slots
        valid = slots < counts[expert]
        pick = order[jnp.minimum(place, assigned - 1)]
        chosen = normed[pick // TOP]
        both = jnp.dot(chosen.astype(jnp.float32), w_gate_up[expert].astype(jnp.float32))
        hidden = (jax.nn.silu(both[:, :FF]) * both[:, FF:]).astype(jnp.bfloat16)
        result = jnp.dot(hidden.astype(jnp.float32), w_down[expert].astype(jnp.float32)).astype(jnp.bfloat16)
        target = jnp.where(valid, pick, assigned)
        return (carry.at[target].set(result, mode='drop'), None)
    outputs, _ = lax.scan(run_expert, jnp.zeros((assigned, D), jnp.bfloat16), jnp.arange(EXPERTS, dtype=jnp.int32))
    blended = jnp.einsum('tkd,tk->td', outputs.reshape(TOKENS, TOP, D).astype(jnp.float32), mix_weights.astype(jnp.float32))
    return (hidden_state + blended).astype(jnp.bfloat16)
```

```python
import functools

import jax
import jax.numpy as jnp
from jax import lax
from jax.experimental import pallas as pl
from jax.experimental.pallas import tpu as pltpu
from jax.sharding import PartitionSpec as P

D = 2048
QH = 32
KVH = 4
HD = 128


def clip_index(clip_lengths, places):
    ends = jnp.cumsum(clip_lengths)
    return jnp.sum((places[:, None] >= ends[None, :]).astype(jnp.int32), axis=1)


def moe_kernel(
    n_z,
    n_experts,
    parts,
    send_ref,
    hidden_ref,
    wgu_hbm,
    wd_hbm,
    out_ref,
    held,
    wgu,
    wd,
    term,
    pair_in,
    relay_x,
    relay_y,
    from_x,
    from_y,
    from_z,
    w_sem,
    z_send,
    z_recv,
    x_send,
    x_recv,
    y_send,
    y_recv,
    da_send,
    da_recv,
    db_send,
    db_recv,
    sib_send,
    sib_recv,
    r_send,
    r_recv,
    rz_send,
    rz_recv,
):
    ep = lax.axis_index("ep")
    tp = lax.axis_index("tp")
    z, y = ep // 2, ep % 2
    x, c = tp // 2, tp % 2
    rows = send_ref.shape[0]
    half = hidden_ref.shape[1]
    cut = half // 2
    width = send_ref.shape[1]
    first, second, rest = pl.ds(0, cut), pl.ds(cut, cut), pl.ds(cut, width - cut)
    x_peer = (ep, (1 - x) * 2 + c)
    y_peer = (z * 2 + 1 - y, tp)
    sib = (ep, x * 2 + 1 - c)
    q_own, q_x = x * 2 + y, (1 - x) * 2 + y
    q_y, q_d = x * 2 + 1 - y, (1 - x) * 2 + 1 - y

    load_gu = pltpu.make_async_copy(wgu_hbm.at[0], wgu, w_sem.at[0])
    load_d = pltpu.make_async_copy(wd_hbm.at[0], wd, w_sem.at[1])
    load_gu.start()
    load_d.start()

    barrier = pltpu.get_barrier_semaphore()
    for peer in (x_peer, y_peer, sib):
        pl.semaphore_signal(
            barrier,
            inc=1,
            device_id={"ep": peer[0], "tp": peer[1]},
            device_id_type=pl.DeviceIdType.MESH,
        )
    for step in range(1, n_z):
        pl.semaphore_signal(
            barrier,
            inc=1,
            device_id={"ep": ((z + step) % n_z) * 2 + y, "tp": tp},
            device_id_type=pl.DeviceIdType.MESH,
        )

    def remote(src, dst, send, recv, peer):
        return pltpu.make_async_remote_copy(
            src_ref=src,
            dst_ref=dst,
            send_sem=send,
            recv_sem=recv,
            device_id={"ep": peer[0], "tp": peer[1]},
            device_id_type=pl.DeviceIdType.MESH,
        )

    def along_z(block, up):
        there = z + 1 if up else z - 1
        return remote(
            held.at[q_own, c, block],
            held.at[q_own, c, block],
            z_send.at[1 if up else 0, block],
            z_recv.at[block],
            (there * 2 + y, tp),
        )

    def over_x(q, block):
        here = held.at[q, c, block]
        return remote(here, here, x_send.at[block], x_recv.at[block], x_peer)

    def over_y(q, block):
        here = held.at[q, c, block]
        return remote(here, here, y_send.at[block], y_recv.at[block], y_peer)

    def diag_x(q, block):
        here = held.at[q, c, block, :, first]
        return remote(here, here, da_send.at[block], da_recv.at[block], x_peer)

    def diag_y(q, block):
        here = held.at[q, c, block, :, rest]
        return remote(here, here, db_send.at[block], db_recv.at[block], y_peer)

    def share(q, core, slot):
        here = held.at[q, core]
        return remote(here, here, sib_send.at[slot], sib_recv.at[slot], sib)

    held[q_own, c, z] = send_ref[...]
    pl.semaphore_wait(barrier, 3 + n_z - 1)

    def each_at(distance, act):
        if distance == 0:
            act(z, 0)
            return
        pl.when(z - distance >= 0)(lambda: act(z - distance, -1))
        pl.when(z + distance < n_z)(lambda: act(z + distance, 1))

    def arrive_z(block, side):
        if side:
            along_z(block, side < 0).wait_recv()
        if side <= 0:
            pl.when(z + 1 < n_z)(lambda: along_z(block, True).start())
        if side >= 0:
            pl.when(z >= 1)(lambda: along_z(block, False).start())
        over_x(q_own, block).start()
        over_y(q_own, block).start()

    def arrive_xy(block, side):
        over_x(q_x, block).wait_recv()
        diag_y(q_x, block).start()
        over_y(q_y, block).wait_recv()
        diag_x(q_y, block).start()

    for distance in range(n_z + 1):
        if distance < n_z:
            each_at(distance, arrive_z)
        if distance == n_z - 1:
            share(q_own, c, 0).start()
        if distance >= 1:
            each_at(distance - 1, arrive_xy)
    share(q_x, c, 1).start()
    share(q_y, c, 2).start()
    load_gu.wait()
    load_d.wait()

    mine = ep * lax.axis_size("tp") + tp
    many = 2 * n_z * rows

    def compute(q):
        both = jnp.dot(
            held[q, :, :, :, 0:half].reshape(many, half),
            wgu[...],
            preferred_element_type=jnp.float32,
        )
        ff = both.shape[1] // 2
        gate, up = both[:, :ff], both[:, ff:]
        acted = (gate / (1.0 + jnp.exp(-gate)) * up).astype(jnp.bfloat16)
        shares = held[q, :, :, :, half:width].reshape(many, width - half).astype(jnp.float32)
        lane = lax.broadcasted_iota(jnp.int32, shares.shape, 1)
        wanted = lane == mine
        for part in range(1, parts):
            wanted = wanted | (lane == mine + part * n_experts)
        mix = jnp.sum(jnp.where(wanted, shares, 0.0), axis=1, keepdims=True)
        tile = half // 4
        for at in range(0, half, tile):
            result = jnp.dot(
                acted, wd[:, at : at + tile], preferred_element_type=jnp.float32
            ).astype(jnp.bfloat16)
            term[q, :, :, at : at + tile] = (
                (result.astype(jnp.float32) * mix)
                .astype(jnp.bfloat16)
                .reshape(2, n_z * rows, tile)
            )

    def pair(q, slot):
        return remote(
            term.at[q, 1 - c], pair_in.at[slot], sib_send.at[4 + slot], sib_recv.at[4 + slot], sib
        )

    def add_pair(q, slot):
        pair(q, slot).wait_recv()
        for at in range(0, half, cut):
            to = pl.ds(at, cut)
            term[q, c, :, to] = (
                term[q, c, :, to].astype(jnp.float32) + pair_in[slot, :, to].astype(jnp.float32)
            ).astype(jnp.bfloat16)

    def reduce_x(q, columns, into, slot):
        return remote(term.at[q, c, :, columns], into, r_send.at[slot], r_recv.at[slot], x_peer)

    def reduce_y(q, columns, into, slot):
        return remote(term.at[q, c, :, columns], into, r_send.at[slot], r_recv.at[slot], y_peer)

    own_x = reduce_x(q_x, first, from_x.at[0], 0)
    own_y = reduce_y(q_y, second, from_y.at[1], 1)
    pass_x = reduce_x(q_d, first, relay_x, 2)
    pass_y = reduce_y(q_d, second, relay_y, 3)
    last_x = reduce_x(q_x, second, from_x.at[1], 4)
    last_y = reduce_y(q_y, first, from_y.at[0], 5)

    share(q_own, 1 - c, 0).wait_recv()
    compute(q_own)
    pair(q_own, 0).start()
    share(q_x, 1 - c, 1).wait_recv()
    compute(q_x)
    pair(q_x, 1).start()
    for block in range(n_z):
        diag_x(q_d, block).wait_recv()
        diag_y(q_d, block).wait_recv()
    share(q_d, c, 3).start()
    share(q_y, 1 - c, 2).wait_recv()
    compute(q_y)
    pair(q_y, 2).start()
    add_pair(q_x, 1)
    own_x.start()
    share(q_d, 1 - c, 3).wait_recv()
    compute(q_d)
    pair(q_d, 3).start()
    add_pair(q_y, 2)
    own_y.start()
    add_pair(q_d, 3)
    pass_x.start()
    pass_y.start()
    add_pair(q_own, 0)

    pass_x.wait_recv()
    term[q_y, c, :, first] = (
        term[q_y, c, :, first].astype(jnp.float32) + relay_x[...].astype(jnp.float32)
    ).astype(jnp.bfloat16)
    last_y.start()
    pass_y.wait_recv()
    term[q_x, c, :, second] = (
        term[q_x, c, :, second].astype(jnp.float32) + relay_y[...].astype(jnp.float32)
    ).astype(jnp.bfloat16)
    last_x.start()

    def finish(number, columns):
        term[q_own, c, :, columns] = (
            term[q_own, c, :, columns].astype(jnp.float32)
            + from_x[number].astype(jnp.float32)
            + from_y[number].astype(jnp.float32)
        ).astype(jnp.bfloat16)

    def deliver(number, columns, step):
        there = (z + step) % n_z
        return remote(
            term.at[q_own, c, pl.ds(pl.multiple_of(there * rows, rows), rows), columns],
            from_z.at[number, n_z - 1 - step],
            rz_send.at[number, step - 1],
            rz_recv.at[number, n_z - 1 - step],
            (there * 2 + y, tp),
        )

    def collect(number, columns):
        total = hidden_ref[:, columns] + term[
            q_own, c, pl.ds(pl.multiple_of(z * rows, rows), rows), columns
        ].astype(jnp.float32)
        for slot in range(n_z - 1):
            remote(
                from_z.at[number, slot],
                from_z.at[number, slot],
                rz_send.at[number, slot],
                rz_recv.at[number, slot],
                sib,
            ).wait_recv()
            total = total + from_z[number, slot].astype(jnp.float32)
        out_ref[:, columns] = total.astype(jnp.bfloat16)

    own_x.wait_recv()
    last_y.wait_recv()
    finish(0, first)
    for step in range(1, n_z):
        deliver(0, first, step).start()
    own_y.wait_recv()
    last_x.wait_recv()
    finish(1, second)
    for step in range(1, n_z):
        deliver(1, second, step).start()
    collect(0, first)
    collect(1, second)

    for copy in (own_x, own_y, pass_x, pass_y, last_x, last_y):
        copy.wait_send()
    for slot, q in enumerate((q_own, q_x, q_y, q_d)):
        share(q, c, slot).wait_send()
        pair(q, slot).wait_send()
    for step in range(1, n_z):
        deliver(0, first, step).wait_send()
        deliver(1, second, step).wait_send()
    for block in range(n_z):
        over_x(q_own, block).wait_send()
        over_y(q_own, block).wait_send()
        diag_x(q_y, block).wait_send()
        diag_y(q_x, block).wait_send()
        pl.when((z + 1 < n_z) & (block <= z))(lambda: along_z(block, True).wait_send())
        pl.when((z >= 1) & (block >= z))(lambda: along_z(block, False).wait_send())


def routed_experts(normed, hidden_state, w_gate_up, w_down, expert_ids, mix_weights):
    n_z = lax.axis_size("ep") // 2
    n_experts = lax.axis_size("ep") * lax.axis_size("tp")
    rows, half = normed.shape
    marks = expert_ids[:, :, None] == jnp.arange(n_experts, dtype=jnp.int32)
    shares = jnp.sum(jnp.where(marks, mix_weights[:, :, None], 0.0), axis=1)
    pieces, left = [], shares
    for _ in range(3):
        piece = lax.reduce_precision(left, 8, 7)
        pieces.append(piece.astype(jnp.bfloat16))
        left = left - piece
    parts = len(pieces)
    spare = -(parts * n_experts) % 128
    pieces.append(jnp.zeros((rows, spare), jnp.bfloat16))
    sent = jnp.concatenate([normed] + pieces, axis=1)
    width = sent.shape[1]
    many = n_z * rows
    cut = half // 2
    dma = pltpu.SemaphoreType.DMA
    return pl.pallas_call(
        functools.partial(moe_kernel, n_z, n_experts, parts),
        out_shape=jax.ShapeDtypeStruct((rows, half), jnp.bfloat16),
        in_specs=[pl.BlockSpec(memory_space=pltpu.VMEM)] * 2
        + [pl.BlockSpec(memory_space=pl.ANY)] * 2,
        out_specs=pl.BlockSpec(memory_space=pltpu.VMEM),
        scratch_shapes=[
            pltpu.VMEM((4, 2, n_z, rows, width), jnp.bfloat16),
            pltpu.VMEM(w_gate_up.shape[1:], jnp.bfloat16),
            pltpu.VMEM(w_down.shape[1:], jnp.bfloat16),
            pltpu.VMEM((4, 2, many, half), jnp.bfloat16),
            pltpu.VMEM((4, many, half), jnp.bfloat16),
            pltpu.VMEM((many, cut), jnp.bfloat16),
            pltpu.VMEM((many, cut), jnp.bfloat16),
            pltpu.VMEM((2, many, cut), jnp.bfloat16),
            pltpu.VMEM((2, many, cut), jnp.bfloat16),
            pltpu.VMEM((2, n_z - 1, rows, cut), jnp.bfloat16),
            dma((2,)),
            dma((2, n_z)),
            dma((n_z,)),
            dma((n_z,)),
            dma((n_z,)),
            dma((n_z,)),
            dma((n_z,)),
            dma((n_z,)),
            dma((n_z,)),
            dma((n_z,)),
            dma((n_z,)),
            dma((8,)),
            dma((8,)),
            dma((6,)),
            dma((6,)),
            dma((2, n_z - 1)),
            dma((2, n_z - 1)),
        ],
        compiler_params=pltpu.CompilerParams(
            collective_id=0, has_side_effects=True, vmem_limit_bytes=44 * 1024 * 1024
        ),
    )(sent, hidden_state, w_gate_up, w_down)


def body(
    queries,
    keys_values,
    residual,
    norm_gain,
    w_out,
    w_gate_up,
    w_down,
    expert_ids,
    mix_weights,
    clip_lengths,
):
    rows = queries.shape[0]
    heads_here = queries.shape[1] // HD
    pool_size = lax.axis_size("pool")
    tensor_size = lax.axis_size("tp")
    context_size = lax.axis_size("ep")
    pool_index = lax.axis_index("pool")
    tensor_index = lax.axis_index("tp")
    pair_heads = keys_values.shape[1] // (2 * HD)
    group = QH // KVH
    head_pick = (
        pool_index * tensor_size + tensor_index
    ) * heads_here // group - pool_index * pair_heads
    own_pairs = lax.dynamic_slice_in_dim(keys_values, head_pick * (2 * HD), 2 * HD, 1)
    places = lax.axis_index("ep") * rows + jnp.arange(rows, dtype=jnp.int32)
    query_clip = clip_index(clip_lengths, places)
    query_heads = queries.reshape(rows, heads_here, HD)
    scale = HD ** (-0.5)
    start_state = (
        jnp.full((heads_here, rows), -1e30, jnp.float32),
        jnp.zeros((heads_here, rows), jnp.float32),
        jnp.zeros((heads_here, rows, HD), jnp.float32),
    )
    piece = lax.all_gather(own_pairs, "ep", axis=0, tiled=True)
    length = piece.shape[0]
    stride = min(length, rows * max(1, 512 // rows))
    while length % stride:
        stride = stride - 1

    def one_block(index, state):
        top, total, numer = state
        block = lax.dynamic_slice_in_dim(piece, index * stride, stride, 0)
        key_clip = clip_index(clip_lengths, index * stride + jnp.arange(stride, dtype=jnp.int32))
        scores = (
            jnp.einsum(
                "rhd,nd->hrn", query_heads, block[:, :HD], preferred_element_type=jnp.float32
            )
            * scale
        )
        same = (query_clip[:, None] == key_clip[None, :])[None, :, :]
        new_top = jnp.maximum(top, jnp.max(jnp.where(same, scores, -1e30), axis=2))
        weights = jnp.where(same, jnp.exp(scores - new_top[:, :, None]), 0.0)
        factor = jnp.exp(top - new_top)
        total = total * factor + jnp.sum(weights, axis=2)
        numer = numer * factor[:, :, None] + jnp.einsum(
            "hrn,nd->hrd",
            weights.astype(jnp.bfloat16),
            block[:, HD:],
            preferred_element_type=jnp.float32,
        )
        return (new_top, total, numer)

    top, total, numer = lax.fori_loop(0, length // stride, one_block, start_state)
    attended = (numer / total[:, :, None]).astype(jnp.bfloat16)
    half = residual.shape[1]
    out_heads = w_out.reshape(heads_here, HD, pool_size * half)
    moe_rows = residual.shape[0]
    start = jnp.int32(0)
    pieces = []
    for offset in range(lax.axis_size(("pool", "tp")) * moe_rows // rows):
        part = start // rows + offset
        weights = lax.dynamic_slice_in_dim(out_heads, part * half, half, 2)
        pieces.append(
            jnp.einsum("hrd,hde->re", attended, weights, preferred_element_type=jnp.float32)
        )
    mixed = lax.psum_scatter(
        jnp.concatenate(pieces, axis=0).astype(jnp.bfloat16),
        ("pool", "tp"),
        scatter_dimension=0,
        tiled=True,
    ).astype(jnp.float32)
    hidden_state = residual.astype(jnp.float32) + mixed
    squares = lax.psum(jnp.sum(hidden_state * hidden_state, axis=1), "pool")
    normed = (hidden_state * lax.rsqrt(squares / D + 1e-06)[:, None] * norm_gain[None, :]).astype(
        jnp.bfloat16
    )
    if (
        pool_size == 1
        and tensor_size == 4
        and context_size % 2 == 0
        and context_size > 2
        and w_gate_up.shape[0] == 1
        and moe_rows % 16 == 0
        and half % 1024 == 0
    ):
        return routed_experts(
            normed, hidden_state, w_gate_up, w_down, expert_ids, mix_weights
        )
    top_k = expert_ids.shape[1]
    local_experts = w_gate_up.shape[0]
    experts = local_experts * context_size * tensor_size
    capacity = 2 * moe_rows * top_k // experts
    flat = expert_ids.reshape(-1)
    marks = (flat[:, None] == jnp.arange(experts, dtype=jnp.int32)[None, :]).astype(jnp.int32)
    rank = jnp.sum(jnp.cumsum(marks, axis=0) * marks, axis=1) - 1
    slot = flat * capacity + rank
    source = jnp.arange(moe_rows * top_k, dtype=jnp.int32) // top_k
    outgoing = jnp.zeros((experts * capacity, half), jnp.bfloat16).at[slot].set(normed[source])
    hidden_width = w_down.shape[1]
    shaped = outgoing.reshape(experts, capacity, half)
    arrived = lax.all_to_all(shaped, ("ep", "tp"), split_axis=0, concat_axis=0, tiled=True)
    width = arrived.shape[1]
    grouped = arrived.reshape(-1, local_experts, width, half)
    both = jnp.einsum("slcd,ldf->slcf", grouped, w_gate_up, preferred_element_type=jnp.float32)
    both = lax.psum(both.astype(jnp.bfloat16), "pool").astype(jnp.float32)
    hidden = (jax.nn.silu(both[..., :hidden_width]) * both[..., hidden_width:]).astype(jnp.bfloat16)
    result = jnp.einsum(
        "slcf,lfd->slcd", hidden, w_down, preferred_element_type=jnp.float32
    ).astype(jnp.bfloat16)
    finished = result.reshape(-1, width, half)
    back = lax.all_to_all(finished, ("ep", "tp"), split_axis=0, concat_axis=0, tiled=True)
    back_rows = back.reshape(experts * capacity, half)[slot]
    gathered = back_rows.reshape(moe_rows, top_k, half).astype(jnp.float32)
    blended = jnp.sum(gathered * mix_weights[:, :, None], axis=1)
    return (hidden_state + blended).astype(jnp.bfloat16)


def solution(mesh):
    placed = (
        P(("grp", "ep"), ("pool", "tp")),
        P(("grp", "ep"), "pool"),
        P(("grp", "ep", "tp"), "pool"),
        P("pool"),
        P(("pool", "tp"), None),
        P(("ep", "tp"), "pool", None),
        P(("ep", "tp"), None, "pool"),
        P(("grp", "ep", "tp"), None),
        P(("grp", "ep", "tp"), None),
        P("grp"),
    )
    return jax.shard_map(
        body, mesh=mesh, in_specs=placed, out_specs=P(("grp", "ep", "tp"), "pool"), check_vma=False
    )
```

```python
import functools

import jax
import jax.numpy as jnp
from jax import lax
from jax.experimental import pallas as pl
from jax.experimental.pallas import tpu as pltpu
from jax.sharding import PartitionSpec as P

D = 2048
QH = 32
KVH = 4
HD = 128


def clip_index(clip_lengths, places):
    ends = jnp.cumsum(clip_lengths)
    return jnp.sum((places[:, None] >= ends[None, :]).astype(jnp.int32), axis=1)


def layer_kernel(
    n_z,
    n_experts,
    parts,
    clip_ref,
    queries_ref,
    kv_ref,
    residual_ref,
    gain_ref,
    ids_ref,
    mix_ref,
    wo_hbm,
    wgu_hbm,
    wd_hbm,
    out_ref,
    kv,
    attended,
    proj,
    sib_in,
    x_in,
    hidden_ref,
    wo,
    kz_send,
    kz_recv,
    ky_send,
    ky_recv,
    at_send,
    at_recv,
    held,
    wgu,
    wd,
    term,
    pair_in,
    relay_x,
    relay_y,
    from_x,
    from_y,
    from_z,
    w_sem,
    z_send,
    z_recv,
    x_send,
    x_recv,
    y_send,
    y_recv,
    da_send,
    da_recv,
    db_send,
    db_recv,
    sib_send,
    sib_recv,
    r_send,
    r_recv,
    rz_send,
    rz_recv,
):
    ep = lax.axis_index("ep")
    tp = lax.axis_index("tp")
    z, y = ep // 2, ep % 2
    x, c = tp // 2, tp % 2
    rows, half = residual_ref.shape
    cut = half // 2
    quarter = half // 4
    width = held.shape[4]
    q_rows = queries_ref.shape[0]
    first, second, rest = pl.ds(0, cut), pl.ds(cut, cut), pl.ds(cut, width - cut)
    x_peer = (ep, (1 - x) * 2 + c)
    y_peer = (z * 2 + 1 - y, tp)
    sib = (ep, x * 2 + 1 - c)
    q_own, q_x = x * 2 + y, (1 - x) * 2 + y
    q_y, q_d = x * 2 + 1 - y, (1 - x) * 2 + 1 - y

    load_o = pltpu.make_async_copy(wo_hbm, wo, w_sem.at[2])
    load_gu = pltpu.make_async_copy(wgu_hbm.at[0], wgu, w_sem.at[0])
    load_d = pltpu.make_async_copy(wd_hbm.at[0], wd, w_sem.at[1])
    load_o.start()
    load_gu.start()
    load_d.start()

    barrier = pltpu.get_barrier_semaphore()
    for peer in (x_peer, y_peer, sib):
        pl.semaphore_signal(
            barrier,
            inc=1,
            device_id={"ep": peer[0], "tp": peer[1]},
            device_id_type=pl.DeviceIdType.MESH,
        )
    for step in range(1, n_z):
        pl.semaphore_signal(
            barrier,
            inc=1,
            device_id={"ep": ((z + step) % n_z) * 2 + y, "tp": tp},
            device_id_type=pl.DeviceIdType.MESH,
        )

    def remote(src, dst, send, recv, peer):
        return pltpu.make_async_remote_copy(
            src_ref=src,
            dst_ref=dst,
            send_sem=send,
            recv_sem=recv,
            device_id={"ep": peer[0], "tp": peer[1]},
            device_id_type=pl.DeviceIdType.MESH,
        )

    def along_z(block, up):
        there = z + 1 if up else z - 1
        return remote(
            held.at[q_own, c, block],
            held.at[q_own, c, block],
            z_send.at[1 if up else 0, block],
            z_recv.at[block],
            (there * 2 + y, tp),
        )

    def over_x(q, block):
        here = held.at[q, c, block]
        return remote(here, here, x_send.at[block], x_recv.at[block], x_peer)

    def over_y(q, block):
        here = held.at[q, c, block]
        return remote(here, here, y_send.at[block], y_recv.at[block], y_peer)

    def diag_x(q, block):
        here = held.at[q, c, block, :, first]
        return remote(here, here, da_send.at[block], da_recv.at[block], x_peer)

    def diag_y(q, block):
        here = held.at[q, c, block, :, rest]
        return remote(here, here, db_send.at[block], db_recv.at[block], y_peer)

    def share(q, core, slot):
        here = held.at[q, core]
        return remote(here, here, sib_send.at[slot], sib_recv.at[slot], sib)

    def each_at(distance, act):
        if distance == 0:
            act(z, 0)
            return
        pl.when(z - distance >= 0)(lambda: act(z - distance, -1))
        pl.when(z + distance < n_z)(lambda: act(z + distance, 1))

    def keys_z(block, up):
        there = z + 1 if up else z - 1
        here = kv.at[block * 2 + y]
        return remote(
            here, here, kz_send.at[1 if up else 0, block], kz_recv.at[block], (there * 2 + y, tp)
        )

    def keys_y(block, side_y):
        here = kv.at[block * 2 + side_y]
        return remote(here, here, ky_send.at[block], ky_recv.at[block], y_peer)

    def keys_arrive(block, side):
        if side:
            keys_z(block, side < 0).wait_recv()
        if side <= 0:
            pl.when(z + 1 < n_z)(lambda: keys_z(block, True).start())
        if side >= 0:
            pl.when(z >= 1)(lambda: keys_z(block, False).start())
        keys_y(block, y).start()

    pair_width = kv.shape[2]
    head = pair_width // 2
    kv[ep] = kv_ref[:, pl.ds(pl.multiple_of(tp * pair_width, pair_width), pair_width)]
    pl.semaphore_wait(barrier, 3 + n_z - 1)
    for distance in range(n_z):
        each_at(distance, keys_arrive)

    n_keys = 2 * n_z * q_rows
    place = lax.broadcasted_iota(jnp.int32, (2 * q_rows, 1), 0)
    place = jnp.where(place >= q_rows, place - q_rows, place) + ep * q_rows
    key_place = lax.broadcasted_iota(jnp.int32, (1, n_keys), 1)
    clip = jnp.zeros(place.shape, jnp.int32)
    key_clip = jnp.zeros(key_place.shape, jnp.int32)
    end = jnp.int32(0)
    for number in range(clip_ref.shape[0]):
        end = end + clip_ref[number]
        clip = clip + jnp.where(place >= end, 1, 0)
        key_clip = key_clip + jnp.where(key_place >= end, 1, 0)
    same = clip == key_clip

    lane = lax.broadcasted_iota(jnp.int32, (rows, width - half), 1)
    base = jnp.zeros(lane.shape, jnp.int32)
    for part in range(1, parts):
        base = base + jnp.where(lane >= part * n_experts, n_experts, 0)
    wanted = lane - base
    weight = jnp.zeros(lane.shape, jnp.float32)
    for slot in range(ids_ref.shape[1]):
        weight = weight + jnp.where(
            ids_ref[:, slot : slot + 1] == wanted, mix_ref[:, slot : slot + 1], 0.0
        )
    packed = jnp.zeros(lane.shape, jnp.float32)
    for part in range(parts):
        piece = weight.astype(jnp.bfloat16).astype(jnp.float32)
        packed = jnp.where(base == part * n_experts, piece, packed)
        weight = weight - piece
    held[q_own, c, z, :, half:width] = packed.astype(jnp.bfloat16)

    for block in range(n_z):
        keys_y(block, 1 - y).wait_recv()
    keys = kv[:, :, 0:head].reshape(n_keys, head)
    values = kv[:, :, head:pair_width].reshape(n_keys, head)
    scale = head ** (-0.5)
    for at in range(0, queries_ref.shape[1], 2 * head):
        two = jnp.concatenate(
            [queries_ref[:, at : at + head], queries_ref[:, at + head : at + 2 * head]], axis=0
        )
        scores = lax.dot_general(
            two, keys, (((1,), (1,)), ((), ())), preferred_element_type=jnp.float32
        )
        scores = jnp.where(same, scores * scale, -1e30)
        top = jnp.max(scores, axis=1, keepdims=True)
        weights = jnp.exp(scores - top)
        total = jnp.sum(weights, axis=1, keepdims=True)
        numer = jnp.dot(
            weights.astype(jnp.bfloat16), values, preferred_element_type=jnp.float32
        )
        result = (numer / total).astype(jnp.bfloat16)
        attended[:, at : at + head] = result[0:q_rows]
        attended[:, at + head : at + 2 * head] = result[q_rows : 2 * q_rows]

    def proj_pair(part):
        columns = pl.ds(part * cut, cut)
        return remote(
            proj.at[1 - c, :, :, columns],
            sib_in.at[:, :, columns],
            at_send.at[part],
            at_recv.at[part],
            sib,
        )

    def proj_x(part):
        columns = pl.ds(part * cut, cut)
        return remote(
            proj.at[c, 1 - x, :, columns],
            x_in.at[:, columns],
            at_send.at[2 + part],
            at_recv.at[2 + part],
            x_peer,
        )

    load_o.wait()
    for part in range(2):
        for at in range(part * cut, (part + 1) * cut, quarter):
            result = jnp.dot(
                attended[...], wo[:, at : at + quarter], preferred_element_type=jnp.float32
            ).astype(jnp.bfloat16)
            for side_x in range(2):
                for side_c in range(2):
                    start = (side_x * 2 + side_c) * rows
                    proj[side_c, side_x, :, at : at + quarter] = result[start : start + rows]
        proj_pair(part).start()
    for part in range(2):
        columns = pl.ds(part * cut, cut)
        proj_pair(part).wait_recv()
        proj[c, 1 - x, :, columns] = (
            proj[c, 1 - x, :, columns].astype(jnp.float32)
            + sib_in[1 - x, :, columns].astype(jnp.float32)
        ).astype(jnp.bfloat16)
        proj_x(part).start()
    for part in range(2):
        columns = pl.ds(part * cut, cut)
        hidden_ref[:, columns] = (
            residual_ref[:, columns].astype(jnp.float32)
            + proj[c, x, :, columns].astype(jnp.float32)
            + sib_in[x, :, columns].astype(jnp.float32)
        )
    for part in range(2):
        columns = pl.ds(part * cut, cut)
        proj_x(part).wait_recv()
        hidden_ref[:, columns] += x_in[:, columns].astype(jnp.float32)
    hidden = hidden_ref[...]
    squares = jnp.sum(hidden * hidden, axis=1, keepdims=True) / half
    held[q_own, c, z, :, 0:half] = (hidden * lax.rsqrt(squares + 1e-06) * gain_ref[...]).astype(
        jnp.bfloat16
    )

    def arrive_z(block, side):
        if side:
            along_z(block, side < 0).wait_recv()
        if side <= 0:
            pl.when(z + 1 < n_z)(lambda: along_z(block, True).start())
        if side >= 0:
            pl.when(z >= 1)(lambda: along_z(block, False).start())
        over_x(q_own, block).start()
        over_y(q_own, block).start()

    def arrive_xy(block, side):
        over_x(q_x, block).wait_recv()
        diag_y(q_x, block).start()
        over_y(q_y, block).wait_recv()
        diag_x(q_y, block).start()

    for distance in range(n_z + 1):
        if distance < n_z:
            each_at(distance, arrive_z)
        if distance == n_z - 1:
            share(q_own, c, 0).start()
        if distance >= 1:
            each_at(distance - 1, arrive_xy)
    share(q_x, c, 1).start()
    share(q_y, c, 2).start()
    load_gu.wait()
    load_d.wait()

    mine = ep * lax.axis_size("tp") + tp
    many = 2 * n_z * rows

    def compute(q):
        both = jnp.dot(
            held[q, :, :, :, 0:half].reshape(many, half),
            wgu[...],
            preferred_element_type=jnp.float32,
        )
        ff = both.shape[1] // 2
        gate, up = both[:, :ff], both[:, ff:]
        acted = (gate / (1.0 + jnp.exp(-gate)) * up).astype(jnp.bfloat16)
        shares = held[q, :, :, :, half:width].reshape(many, width - half).astype(jnp.float32)
        lane = lax.broadcasted_iota(jnp.int32, shares.shape, 1)
        wanted = lane == mine
        for part in range(1, parts):
            wanted = wanted | (lane == mine + part * n_experts)
        mix = jnp.sum(jnp.where(wanted, shares, 0.0), axis=1, keepdims=True)
        tile = half // 4
        for at in range(0, half, tile):
            result = jnp.dot(
                acted, wd[:, at : at + tile], preferred_element_type=jnp.float32
            ).astype(jnp.bfloat16)
            term[q, :, :, at : at + tile] = (
                (result.astype(jnp.float32) * mix)
                .astype(jnp.bfloat16)
                .reshape(2, n_z * rows, tile)
            )

    def pair(q, slot):
        return remote(
            term.at[q, 1 - c], pair_in.at[slot], sib_send.at[4 + slot], sib_recv.at[4 + slot], sib
        )

    def add_pair(q, slot):
        pair(q, slot).wait_recv()
        for at in range(0, half, cut):
            to = pl.ds(at, cut)
            term[q, c, :, to] = (
                term[q, c, :, to].astype(jnp.float32) + pair_in[slot, :, to].astype(jnp.float32)
            ).astype(jnp.bfloat16)

    def reduce_x(q, columns, into, slot):
        return remote(term.at[q, c, :, columns], into, r_send.at[slot], r_recv.at[slot], x_peer)

    def reduce_y(q, columns, into, slot):
        return remote(term.at[q, c, :, columns], into, r_send.at[slot], r_recv.at[slot], y_peer)

    low = [pl.ds(0, quarter), pl.ds(quarter, quarter)]
    high = [pl.ds(cut, quarter), pl.ds(cut + quarter, quarter)]
    own_x = reduce_x(q_x, first, from_x.at[0], 0)
    own_y = reduce_y(q_y, second, from_y.at[1], 1)
    pass_x = [reduce_x(q_d, low[i], relay_x.at[:, low[i]], 2 + i) for i in range(2)]
    pass_y = [reduce_y(q_d, high[i], relay_y.at[:, low[i]], 4 + i) for i in range(2)]
    last_x = [reduce_x(q_x, high[i], from_x.at[1, :, low[i]], 6 + i) for i in range(2)]
    last_y = [reduce_y(q_y, low[i], from_y.at[0, :, low[i]], 8 + i) for i in range(2)]

    share(q_own, 1 - c, 0).wait_recv()
    compute(q_own)
    pair(q_own, 0).start()
    share(q_x, 1 - c, 1).wait_recv()
    compute(q_x)
    pair(q_x, 1).start()
    for block in range(n_z):
        diag_x(q_d, block).wait_recv()
        diag_y(q_d, block).wait_recv()
    share(q_d, c, 3).start()
    share(q_y, 1 - c, 2).wait_recv()
    compute(q_y)
    pair(q_y, 2).start()
    add_pair(q_x, 1)
    own_x.start()
    share(q_d, 1 - c, 3).wait_recv()
    compute(q_d)
    pair(q_d, 3).start()
    add_pair(q_y, 2)
    own_y.start()
    add_pair(q_d, 3)
    for i in range(2):
        pass_x[i].start()
        pass_y[i].start()
    add_pair(q_own, 0)

    for i in range(2):
        pass_x[i].wait_recv()
        term[q_y, c, :, low[i]] = (
            term[q_y, c, :, low[i]].astype(jnp.float32) + relay_x[:, low[i]].astype(jnp.float32)
        ).astype(jnp.bfloat16)
        last_y[i].start()
        pass_y[i].wait_recv()
        term[q_x, c, :, high[i]] = (
            term[q_x, c, :, high[i]].astype(jnp.float32) + relay_y[:, low[i]].astype(jnp.float32)
        ).astype(jnp.bfloat16)
        last_x[i].start()

    def finish(side, i):
        columns = high[i] if side else low[i]
        term[q_own, c, :, columns] = (
            term[q_own, c, :, columns].astype(jnp.float32)
            + from_x[side, :, low[i]].astype(jnp.float32)
            + from_y[side, :, low[i]].astype(jnp.float32)
        ).astype(jnp.bfloat16)

    def deliver(side, i, step):
        there = (z + step) % n_z
        return remote(
            term.at[
                q_own,
                c,
                pl.ds(pl.multiple_of(there * rows, rows), rows),
                high[i] if side else low[i],
            ],
            from_z.at[side, i, n_z - 1 - step],
            rz_send.at[side, i, step - 1],
            rz_recv.at[side, i, n_z - 1 - step],
            (there * 2 + y, tp),
        )

    def collect(side, i):
        columns = high[i] if side else low[i]
        total = hidden_ref[:, columns] + term[
            q_own, c, pl.ds(pl.multiple_of(z * rows, rows), rows), columns
        ].astype(jnp.float32)
        for step in range(1, n_z):
            deliver(side, i, step).wait_recv()
            total = total + from_z[side, i, n_z - 1 - step].astype(jnp.float32)
        out_ref[:, columns] = total.astype(jnp.bfloat16)

    own_x.wait_recv()
    own_y.wait_recv()
    for i in range(2):
        for side in range(2):
            (last_x if side else last_y)[i].wait_recv()
            finish(side, i)
            for step in range(1, n_z):
                deliver(side, i, step).start()
    for i in range(2):
        for side in range(2):
            collect(side, i)

    for copy in [own_x, own_y] + pass_x + pass_y + last_x + last_y:
        copy.wait_send()
    for part in range(2):
        proj_pair(part).wait_send()
        proj_x(part).wait_send()
    for slot, q in enumerate((q_own, q_x, q_y, q_d)):
        share(q, c, slot).wait_send()
        pair(q, slot).wait_send()
    for step in range(1, n_z):
        for i in range(2):
            for side in range(2):
                deliver(side, i, step).wait_send()
    for block in range(n_z):
        keys_y(block, y).wait_send()
        pl.when((z + 1 < n_z) & (block <= z))(lambda: keys_z(block, True).wait_send())
        pl.when((z >= 1) & (block >= z))(lambda: keys_z(block, False).wait_send())
        over_x(q_own, block).wait_send()
        over_y(q_own, block).wait_send()
        diag_x(q_y, block).wait_send()
        diag_y(q_x, block).wait_send()
        pl.when((z + 1 < n_z) & (block <= z))(lambda: along_z(block, True).wait_send())
        pl.when((z >= 1) & (block >= z))(lambda: along_z(block, False).wait_send())


def whole_layer(
    queries,
    keys_values,
    residual,
    norm_gain,
    w_out,
    w_gate_up,
    w_down,
    expert_ids,
    mix_weights,
    clip_lengths,
):
    n_ep = lax.axis_size("ep")
    n_z = n_ep // 2
    n_experts = n_ep * lax.axis_size("tp")
    rows, half = residual.shape
    q_rows = queries.shape[0]
    parts = 3
    width = half + -(-parts * n_experts // 128) * 128
    many = n_z * rows
    cut = half // 2
    dma = pltpu.SemaphoreType.DMA
    bf16 = jnp.bfloat16
    in_vmem = pl.BlockSpec(memory_space=pltpu.VMEM)
    return pl.pallas_call(
        functools.partial(layer_kernel, n_z, n_experts, parts),
        out_shape=jax.ShapeDtypeStruct((rows, half), bf16),
        in_specs=[pl.BlockSpec(memory_space=pltpu.SMEM)]
        + [in_vmem] * 6
        + [pl.BlockSpec(memory_space=pl.ANY)] * 3,
        out_specs=in_vmem,
        scratch_shapes=[
            pltpu.VMEM((n_ep, q_rows, 2 * HD), bf16),
            pltpu.VMEM(queries.shape, bf16),
            pltpu.VMEM((2, 2, rows, half), bf16),
            pltpu.VMEM((2, rows, half), bf16),
            pltpu.VMEM((rows, half), bf16),
            pltpu.VMEM((rows, half), jnp.float32),
            pltpu.VMEM(w_out.shape, bf16),
            dma((2, n_z)),
            dma((n_z,)),
            dma((n_z,)),
            dma((n_z,)),
            dma((4,)),
            dma((4,)),
            pltpu.VMEM((4, 2, n_z, rows, width), bf16),
            pltpu.VMEM(w_gate_up.shape[1:], bf16),
            pltpu.VMEM(w_down.shape[1:], bf16),
            pltpu.VMEM((4, 2, many, half), bf16),
            pltpu.VMEM((4, many, half), bf16),
            pltpu.VMEM((many, cut), bf16),
            pltpu.VMEM((many, cut), bf16),
            pltpu.VMEM((2, many, cut), bf16),
            pltpu.VMEM((2, many, cut), bf16),
            pltpu.VMEM((2, 2, n_z - 1, rows, cut // 2), bf16),
            dma((3,)),
            dma((2, n_z)),
        ]
        + [dma((n_z,))] * 9
        + [dma((8,))] * 2
        + [dma((10,))] * 2
        + [dma((2, 2, n_z - 1))] * 2,
        compiler_params=pltpu.CompilerParams(
            collective_id=0, has_side_effects=True, vmem_limit_bytes=48 * 1024 * 1024
        ),
    )(
        clip_lengths,
        queries,
        keys_values,
        residual,
        norm_gain.reshape(1, half),
        expert_ids,
        mix_weights,
        w_out,
        w_gate_up,
        w_down,
    )


def body(
    queries,
    keys_values,
    residual,
    norm_gain,
    w_out,
    w_gate_up,
    w_down,
    expert_ids,
    mix_weights,
    clip_lengths,
):
    rows = queries.shape[0]
    heads_here = queries.shape[1] // HD
    if (
        lax.axis_size("pool") == 1
        and lax.axis_size("tp") == 4
        and lax.axis_size("ep") % 2 == 0
        and lax.axis_size("ep") > 2
        and heads_here == QH // KVH
        and w_gate_up.shape[0] == 1
        and residual.shape[0] % 16 == 0
        and residual.shape[1] == D
        and rows == 4 * residual.shape[0]
    ):
        return whole_layer(
            queries,
            keys_values,
            residual,
            norm_gain,
            w_out,
            w_gate_up,
            w_down,
            expert_ids,
            mix_weights,
            clip_lengths,
        )
    pool_size = lax.axis_size("pool")
    tensor_size = lax.axis_size("tp")
    context_size = lax.axis_size("ep")
    pool_index = lax.axis_index("pool")
    tensor_index = lax.axis_index("tp")
    pair_heads = keys_values.shape[1] // (2 * HD)
    group = QH // KVH
    head_pick = (
        pool_index * tensor_size + tensor_index
    ) * heads_here // group - pool_index * pair_heads
    own_pairs = lax.dynamic_slice_in_dim(keys_values, head_pick * (2 * HD), 2 * HD, 1)
    places = lax.axis_index("ep") * rows + jnp.arange(rows, dtype=jnp.int32)
    query_clip = clip_index(clip_lengths, places)
    query_heads = queries.reshape(rows, heads_here, HD)
    scale = HD ** (-0.5)
    start_state = (
        jnp.full((heads_here, rows), -1e30, jnp.float32),
        jnp.zeros((heads_here, rows), jnp.float32),
        jnp.zeros((heads_here, rows, HD), jnp.float32),
    )
    piece = lax.all_gather(own_pairs, "ep", axis=0, tiled=True)
    length = piece.shape[0]
    stride = min(length, rows * max(1, 512 // rows))
    while length % stride:
        stride = stride - 1

    def one_block(index, state):
        top, total, numer = state
        block = lax.dynamic_slice_in_dim(piece, index * stride, stride, 0)
        key_clip = clip_index(clip_lengths, index * stride + jnp.arange(stride, dtype=jnp.int32))
        scores = (
            jnp.einsum(
                "rhd,nd->hrn", query_heads, block[:, :HD], preferred_element_type=jnp.float32
            )
            * scale
        )
        same = (query_clip[:, None] == key_clip[None, :])[None, :, :]
        new_top = jnp.maximum(top, jnp.max(jnp.where(same, scores, -1e30), axis=2))
        weights = jnp.where(same, jnp.exp(scores - new_top[:, :, None]), 0.0)
        factor = jnp.exp(top - new_top)
        total = total * factor + jnp.sum(weights, axis=2)
        numer = numer * factor[:, :, None] + jnp.einsum(
            "hrn,nd->hrd",
            weights.astype(jnp.bfloat16),
            block[:, HD:],
            preferred_element_type=jnp.float32,
        )
        return (new_top, total, numer)

    top, total, numer = lax.fori_loop(0, length // stride, one_block, start_state)
    attended = (numer / total[:, :, None]).astype(jnp.bfloat16)
    half = residual.shape[1]
    out_heads = w_out.reshape(heads_here, HD, pool_size * half)
    moe_rows = residual.shape[0]
    start = jnp.int32(0)
    pieces = []
    for offset in range(lax.axis_size(("pool", "tp")) * moe_rows // rows):
        part = start // rows + offset
        weights = lax.dynamic_slice_in_dim(out_heads, part * half, half, 2)
        pieces.append(
            jnp.einsum("hrd,hde->re", attended, weights, preferred_element_type=jnp.float32)
        )
    mixed = lax.psum_scatter(
        jnp.concatenate(pieces, axis=0).astype(jnp.bfloat16),
        ("pool", "tp"),
        scatter_dimension=0,
        tiled=True,
    ).astype(jnp.float32)
    hidden_state = residual.astype(jnp.float32) + mixed
    squares = lax.psum(jnp.sum(hidden_state * hidden_state, axis=1), "pool")
    normed = (hidden_state * lax.rsqrt(squares / D + 1e-06)[:, None] * norm_gain[None, :]).astype(
        jnp.bfloat16
    )
    top_k = expert_ids.shape[1]
    local_experts = w_gate_up.shape[0]
    experts = local_experts * context_size * tensor_size
    capacity = 2 * moe_rows * top_k // experts
    flat = expert_ids.reshape(-1)
    marks = (flat[:, None] == jnp.arange(experts, dtype=jnp.int32)[None, :]).astype(jnp.int32)
    rank = jnp.sum(jnp.cumsum(marks, axis=0) * marks, axis=1) - 1
    slot = flat * capacity + rank
    source = jnp.arange(moe_rows * top_k, dtype=jnp.int32) // top_k
    outgoing = jnp.zeros((experts * capacity, half), jnp.bfloat16).at[slot].set(normed[source])
    hidden_width = w_down.shape[1]
    shaped = outgoing.reshape(experts, capacity, half)
    arrived = lax.all_to_all(shaped, ("ep", "tp"), split_axis=0, concat_axis=0, tiled=True)
    width = arrived.shape[1]
    grouped = arrived.reshape(-1, local_experts, width, half)
    both = jnp.einsum("slcd,ldf->slcf", grouped, w_gate_up, preferred_element_type=jnp.float32)
    both = lax.psum(both.astype(jnp.bfloat16), "pool").astype(jnp.float32)
    hidden = (jax.nn.silu(both[..., :hidden_width]) * both[..., hidden_width:]).astype(jnp.bfloat16)
    result = jnp.einsum(
        "slcf,lfd->slcd", hidden, w_down, preferred_element_type=jnp.float32
    ).astype(jnp.bfloat16)
    finished = result.reshape(-1, width, half)
    back = lax.all_to_all(finished, ("ep", "tp"), split_axis=0, concat_axis=0, tiled=True)
    back_rows = back.reshape(experts * capacity, half)[slot]
    gathered = back_rows.reshape(moe_rows, top_k, half).astype(jnp.float32)
    blended = jnp.sum(gathered * mix_weights[:, :, None], axis=1)
    return (hidden_state + blended).astype(jnp.bfloat16)


def solution(mesh):
    placed = (
        P(("grp", "ep"), ("pool", "tp")),
        P(("grp", "ep"), "pool"),
        P(("grp", "ep", "tp"), "pool"),
        P("pool"),
        P(("pool", "tp"), None),
        P(("ep", "tp"), "pool", None),
        P(("ep", "tp"), None, "pool"),
        P(("grp", "ep", "tp"), None),
        P(("grp", "ep", "tp"), None),
        P("grp"),
    )
    return jax.shard_map(
        body, mesh=mesh, in_specs=placed, out_specs=P(("grp", "ep", "tp"), "pool"), check_vma=False
    )
```

```python
import functools
import math

import jax
import jax.numpy as jnp
from jax import lax
from jax.experimental import pallas as pl
from jax.experimental.pallas import tpu as pltpu
from jax.sharding import PartitionSpec as P

D = 2048
QH = 32
KVH = 4
HD = 128


def clip_index(clip_lengths, places):
    ends = jnp.cumsum(clip_lengths)
    return jnp.sum((places[:, None] >= ends[None, :]).astype(jnp.int32), axis=1)


def layer_kernel(
    n_z,
    n_experts,
    parts,
    clip_ref,
    queries_hbm,
    kv_hbm,
    residual_hbm,
    gain_hbm,
    ids_hbm,
    mix_hbm,
    wo_hbm,
    wgu_hbm,
    wd_hbm,
    out_ref,
    queries_ref,
    residual_ref,
    gain_ref,
    ids_ref,
    mix_ref,
    kv,
    attended,
    proj,
    sib_in,
    x_in,
    hidden_ref,
    wo,
    kz_send,
    kz_recv,
    ky_send,
    ky_recv,
    at_send,
    at_recv,
    held,
    wgu,
    wd,
    term,
    pair_in,
    relay_x,
    relay_y,
    from_x,
    from_y,
    from_z,
    w_sem,
    z_send,
    z_recv,
    x_send,
    x_recv,
    y_send,
    y_recv,
    da_send,
    da_recv,
    db_send,
    db_recv,
    sib_send,
    sib_recv,
    pair_send,
    pair_recv,
    r_send,
    r_recv,
    rz_send,
    rz_recv,
):
    ep = lax.axis_index("ep")
    tp = lax.axis_index("tp")
    z, y = ep // 2, ep % 2
    x, c = tp // 2, tp % 2
    rows, half = residual_ref.shape
    cut = half // 2
    quarter = half // 4
    width = held.shape[4]
    q_rows = queries_ref.shape[0]
    first, second, rest = pl.ds(0, cut), pl.ds(cut, cut), pl.ds(cut, width - cut)
    x_peer = (ep, (1 - x) * 2 + c)
    y_peer = (z * 2 + 1 - y, tp)
    sib = (ep, x * 2 + 1 - c)
    q_own, q_x = x * 2 + y, (1 - x) * 2 + y
    q_y, q_d = x * 2 + 1 - y, (1 - x) * 2 + 1 - y

    pair_width = kv.shape[2]
    own_keys = kv_hbm.at[:, pl.ds(pl.multiple_of(tp * pair_width, pair_width), pair_width)]
    loads = [
        pltpu.make_async_copy(src, dst, w_sem.at[number])
        for number, (src, dst) in enumerate(
            (
                (own_keys, kv.at[ep]),
                (queries_hbm, queries_ref),
                (ids_hbm, ids_ref),
                (mix_hbm, mix_ref),
                (residual_hbm, residual_ref),
                (gain_hbm, gain_ref),
                (wo_hbm, wo),
                (wgu_hbm.at[0], wgu),
                (wd_hbm.at[0], wd),
            )
        )
    ]
    for load in loads:
        load.start()

    barrier = pltpu.get_barrier_semaphore()
    for peer in (x_peer, y_peer, sib):
        pl.semaphore_signal(
            barrier,
            inc=1,
            device_id={"ep": peer[0], "tp": peer[1]},
            device_id_type=pl.DeviceIdType.MESH,
        )
    for step in range(1, n_z):
        pl.semaphore_signal(
            barrier,
            inc=1,
            device_id={"ep": ((z + step) % n_z) * 2 + y, "tp": tp},
            device_id_type=pl.DeviceIdType.MESH,
        )

    def remote(src, dst, send, recv, peer):
        return pltpu.make_async_remote_copy(
            src_ref=src,
            dst_ref=dst,
            send_sem=send,
            recv_sem=recv,
            device_id={"ep": peer[0], "tp": peer[1]},
            device_id_type=pl.DeviceIdType.MESH,
        )

    def along_z(block, up):
        there = z + 1 if up else z - 1
        return remote(
            held.at[q_own, c, block],
            held.at[q_own, c, block],
            z_send.at[1 if up else 0, block],
            z_recv.at[block],
            (there * 2 + y, tp),
        )

    def over_x(q, block):
        here = held.at[q, c, block]
        return remote(here, here, x_send.at[block], x_recv.at[block], x_peer)

    def over_y(q, block):
        here = held.at[q, c, block]
        return remote(here, here, y_send.at[block], y_recv.at[block], y_peer)

    def diag_x(q, block):
        here = held.at[q, c, block, :, first]
        return remote(here, here, da_send.at[block], da_recv.at[block], x_peer)

    def diag_y(q, block):
        here = held.at[q, c, block, :, rest]
        return remote(here, here, db_send.at[block], db_recv.at[block], y_peer)

    def share(q, core, slot, block):
        here = held.at[q, core, block]
        return remote(here, here, sib_send.at[slot, block], sib_recv.at[slot, block], sib)

    def shares_arrive(q, slot):
        for block in range(n_z):
            share(q, 1 - c, slot, block).wait_recv()

    def each_at(distance, act):
        if distance == 0:
            act(z, 0)
            return
        pl.when(z - distance >= 0)(lambda: act(z - distance, -1))
        pl.when(z + distance < n_z)(lambda: act(z + distance, 1))

    def keys_z(block, up):
        there = z + 1 if up else z - 1
        here = kv.at[block * 2 + y]
        return remote(
            here, here, kz_send.at[1 if up else 0, block], kz_recv.at[block], (there * 2 + y, tp)
        )

    def keys_y(block, side_y):
        here = kv.at[block * 2 + side_y]
        return remote(here, here, ky_send.at[block], ky_recv.at[block], y_peer)

    def keys_arrive(block, side):
        if side:
            keys_z(block, side < 0).wait_recv()
        if side <= 0:
            pl.when(z + 1 < n_z)(lambda: keys_z(block, True).start())
        if side >= 0:
            pl.when(z >= 1)(lambda: keys_z(block, False).start())
        keys_y(block, y).start()

    head = pair_width // 2
    loads[0].wait()
    pl.semaphore_wait(barrier, 3 + n_z - 1)
    for distance in range(n_z):
        each_at(distance, keys_arrive)

    n_keys = 2 * n_z * q_rows
    place = lax.broadcasted_iota(jnp.int32, (2 * q_rows, 1), 0)
    place = jnp.where(place >= q_rows, place - q_rows, place) + ep * q_rows
    key_place = lax.broadcasted_iota(jnp.int32, (1, n_keys), 1)
    clip = jnp.zeros(place.shape, jnp.int32)
    key_clip = jnp.zeros(key_place.shape, jnp.int32)
    end = jnp.int32(0)
    for number in range(clip_ref.shape[0]):
        end = end + clip_ref[number]
        clip = clip + jnp.where(place >= end, 1, 0)
        key_clip = key_clip + jnp.where(key_place >= end, 1, 0)
    same = clip == key_clip

    loads[2].wait()
    loads[3].wait()
    lane = lax.broadcasted_iota(jnp.int32, (width - half, rows), 0)
    base = jnp.zeros(lane.shape, jnp.int32)
    for part in range(1, parts):
        base = base + jnp.where(lane >= part * n_experts, n_experts, 0)
    wanted = lane - base
    weight = jnp.zeros(lane.shape, jnp.float32)
    for slot in range(ids_ref.shape[0]):
        weight = weight + jnp.where(
            ids_ref[slot : slot + 1, :] == wanted, mix_ref[slot : slot + 1, :], 0.0
        )
    packed = jnp.zeros(lane.shape, jnp.float32)
    for part in range(parts):
        piece = weight.astype(jnp.bfloat16).astype(jnp.float32)
        packed = jnp.where(base == part * n_experts, piece, packed)
        weight = weight - piece
    unit = lax.broadcasted_iota(jnp.int32, (rows, rows), 0) == lax.broadcasted_iota(
        jnp.int32, (rows, rows), 1
    )
    held[q_own, c, z, :, half:width] = lax.dot_general(
        jnp.where(unit, 1.0, 0.0).astype(jnp.bfloat16),
        packed.astype(jnp.bfloat16),
        (((1,), (1,)), ((), ())),
        preferred_element_type=jnp.float32,
    ).astype(jnp.bfloat16)

    loads[1].wait()
    for block in range(n_z):
        keys_y(block, 1 - y).wait_recv()
    keys = kv[:, :, 0:head].reshape(n_keys, head)
    values = kv[:, :, head:pair_width].reshape(n_keys, head)
    scale = head ** (-0.5) * math.log2(math.e)
    for at in range(0, queries_ref.shape[1], 2 * head):
        two = jnp.concatenate(
            [queries_ref[:, at : at + head], queries_ref[:, at + head : at + 2 * head]], axis=0
        )
        scores = lax.dot_general(
            two, keys, (((1,), (1,)), ((), ())), preferred_element_type=jnp.float32
        )
        scores = jnp.where(same, scores, -1e30)
        top = jnp.max(scores, axis=1, keepdims=True)
        weights = jnp.exp2((scores - top) * scale)
        total = jnp.sum(weights, axis=1, keepdims=True)
        numer = jnp.dot(
            weights.astype(jnp.bfloat16), values, preferred_element_type=jnp.float32
        )
        result = (numer / total).astype(jnp.bfloat16)
        attended[:, at : at + head] = result[0:q_rows]
        attended[:, at + head : at + 2 * head] = result[q_rows : 2 * q_rows]

    def proj_pair(part):
        columns = pl.ds(part * cut, cut)
        return remote(
            proj.at[1 - c, :, :, columns],
            sib_in.at[:, :, columns],
            at_send.at[part],
            at_recv.at[part],
            sib,
        )

    def proj_x(part):
        columns = pl.ds(part * cut, cut)
        return remote(
            proj.at[c, 1 - x, :, columns],
            x_in.at[:, columns],
            at_send.at[2 + part],
            at_recv.at[2 + part],
            x_peer,
        )

    loads[6].wait()
    for part in range(2):
        for at in range(part * cut, (part + 1) * cut, quarter):
            result = jnp.dot(
                attended[...], wo[:, at : at + quarter], preferred_element_type=jnp.float32
            ).astype(jnp.bfloat16)
            for side_x in range(2):
                for side_c in range(2):
                    start = (side_x * 2 + side_c) * rows
                    proj[side_c, side_x, :, at : at + quarter] = result[start : start + rows]
        proj_pair(part).start()
    for part in range(2):
        columns = pl.ds(part * cut, cut)
        proj_pair(part).wait_recv()
        proj[c, 1 - x, :, columns] = (
            proj[c, 1 - x, :, columns].astype(jnp.float32)
            + sib_in[1 - x, :, columns].astype(jnp.float32)
        ).astype(jnp.bfloat16)
        proj_x(part).start()
    loads[4].wait()
    loads[5].wait()
    for part in range(2):
        columns = pl.ds(part * cut, cut)
        hidden_ref[:, columns] = (
            residual_ref[:, columns].astype(jnp.float32)
            + proj[c, x, :, columns].astype(jnp.float32)
            + sib_in[x, :, columns].astype(jnp.float32)
        )
    for part in range(2):
        columns = pl.ds(part * cut, cut)
        proj_x(part).wait_recv()
        hidden_ref[:, columns] += x_in[:, columns].astype(jnp.float32)
    hidden = hidden_ref[...]
    squares = jnp.sum(hidden * hidden, axis=1, keepdims=True) / half
    held[q_own, c, z, :, 0:half] = (hidden * lax.rsqrt(squares + 1e-06) * gain_ref[...]).astype(
        jnp.bfloat16
    )

    def arrive_z(block, side):
        if side:
            along_z(block, side < 0).wait_recv()
        if side <= 0:
            pl.when(z + 1 < n_z)(lambda: along_z(block, True).start())
        if side >= 0:
            pl.when(z >= 1)(lambda: along_z(block, False).start())
        over_x(q_own, block).start()
        over_y(q_own, block).start()
        share(q_own, c, 0, block).start()

    def arrive_xy(block, side):
        over_x(q_x, block).wait_recv()
        diag_y(q_x, block).start()
        share(q_x, c, 1, block).start()
        over_y(q_y, block).wait_recv()
        diag_x(q_y, block).start()
        share(q_y, c, 2, block).start()

    def arrive_diag(block, side):
        diag_x(q_d, block).wait_recv()
        diag_y(q_d, block).wait_recv()
        share(q_d, c, 3, block).start()

    for distance in range(n_z + 1):
        if distance < n_z:
            each_at(distance, arrive_z)
        if distance >= 1:
            each_at(distance - 1, arrive_xy)
    loads[7].wait()
    loads[8].wait()

    mine = ep * lax.axis_size("tp") + tp
    many = 2 * n_z * rows

    def pair(q, slot, part):
        columns = pl.ds(part * cut, cut)
        return remote(
            term.at[q, 1 - c, :, columns],
            pair_in.at[slot, :, columns],
            pair_send.at[slot, part],
            pair_recv.at[slot, part],
            sib,
        )

    def compute(q, slot):
        both = jnp.dot(
            held[q, :, :, :, 0:half].reshape(many, half),
            wgu[...],
            preferred_element_type=jnp.float32,
        )
        ff = both.shape[1] // 2
        gate, up = both[:, :ff], both[:, ff:]
        acted = (gate / (1.0 + jnp.exp(-gate)) * up).astype(jnp.bfloat16)
        shares = held[q, :, :, :, half:width].reshape(many, width - half).astype(jnp.float32)
        lane = lax.broadcasted_iota(jnp.int32, shares.shape, 1)
        wanted = lane == mine
        for part in range(1, parts):
            wanted = wanted | (lane == mine + part * n_experts)
        mix = jnp.sum(jnp.where(wanted, shares, 0.0), axis=1, keepdims=True)
        tile = half // 4
        for at in range(0, half, tile):
            result = jnp.dot(
                acted, wd[:, at : at + tile], preferred_element_type=jnp.float32
            ).astype(jnp.bfloat16)
            term[q, :, :, at : at + tile] = (
                (result.astype(jnp.float32) * mix)
                .astype(jnp.bfloat16)
                .reshape(2, n_z * rows, tile)
            )
            if (at + tile) % cut == 0:
                pair(q, slot, at // cut).start()

    def add_pair(q, slot, part):
        pair(q, slot, part).wait_recv()
        to = pl.ds(part * cut, cut)
        term[q, c, :, to] = (
            term[q, c, :, to].astype(jnp.float32) + pair_in[slot, :, to].astype(jnp.float32)
        ).astype(jnp.bfloat16)

    def reduce_x(q, columns, into, slot):
        return remote(term.at[q, c, :, columns], into, r_send.at[slot], r_recv.at[slot], x_peer)

    def reduce_y(q, columns, into, slot):
        return remote(term.at[q, c, :, columns], into, r_send.at[slot], r_recv.at[slot], y_peer)

    low = [pl.ds(0, quarter), pl.ds(quarter, quarter)]
    high = [pl.ds(cut, quarter), pl.ds(cut + quarter, quarter)]
    own_x = reduce_x(q_x, first, from_x.at[0], 0)
    own_y = reduce_y(q_y, second, from_y.at[1], 1)
    pass_x = [reduce_x(q_d, low[i], relay_x.at[:, low[i]], 2 + i) for i in range(2)]
    pass_y = [reduce_y(q_d, high[i], relay_y.at[:, low[i]], 4 + i) for i in range(2)]
    last_x = [reduce_x(q_x, high[i], from_x.at[1, :, low[i]], 6 + i) for i in range(2)]
    last_y = [reduce_y(q_y, low[i], from_y.at[0, :, low[i]], 8 + i) for i in range(2)]

    shares_arrive(q_x, 1)
    compute(q_x, 1)
    shares_arrive(q_y, 2)
    compute(q_y, 2)
    add_pair(q_x, 1, 0)
    own_x.start()
    add_pair(q_y, 2, 1)
    own_y.start()
    for distance in range(n_z):
        each_at(distance, arrive_diag)
    shares_arrive(q_own, 0)
    compute(q_own, 0)
    shares_arrive(q_d, 3)
    compute(q_d, 3)
    add_pair(q_d, 3, 0)
    for copy in pass_x:
        copy.start()
    add_pair(q_d, 3, 1)
    for copy in pass_y:
        copy.start()
    add_pair(q_y, 2, 0)
    add_pair(q_x, 1, 1)
    add_pair(q_own, 0, 0)
    add_pair(q_own, 0, 1)

    for i in range(2):
        pass_x[i].wait_recv()
        term[q_y, c, :, low[i]] = (
            term[q_y, c, :, low[i]].astype(jnp.float32) + relay_x[:, low[i]].astype(jnp.float32)
        ).astype(jnp.bfloat16)
        last_y[i].start()
        pass_y[i].wait_recv()
        term[q_x, c, :, high[i]] = (
            term[q_x, c, :, high[i]].astype(jnp.float32) + relay_y[:, low[i]].astype(jnp.float32)
        ).astype(jnp.bfloat16)
        last_x[i].start()

    def finish(side, i):
        columns = high[i] if side else low[i]
        term[q_own, c, :, columns] = (
            term[q_own, c, :, columns].astype(jnp.float32)
            + from_x[side, :, low[i]].astype(jnp.float32)
            + from_y[side, :, low[i]].astype(jnp.float32)
        ).astype(jnp.bfloat16)

    def deliver(side, i, step):
        there = (z + step) % n_z
        return remote(
            term.at[
                q_own,
                c,
                pl.ds(pl.multiple_of(there * rows, rows), rows),
                high[i] if side else low[i],
            ],
            from_z.at[side, i, n_z - 1 - step],
            rz_send.at[side, i, step - 1],
            rz_recv.at[side, i, n_z - 1 - step],
            (there * 2 + y, tp),
        )

    def collect(side, i):
        columns = high[i] if side else low[i]
        total = hidden_ref[:, columns] + term[
            q_own, c, pl.ds(pl.multiple_of(z * rows, rows), rows), columns
        ].astype(jnp.float32)
        for step in range(1, n_z):
            deliver(side, i, step).wait_recv()
            total = total + from_z[side, i, n_z - 1 - step].astype(jnp.float32)
        out_ref[:, columns] = total.astype(jnp.bfloat16)

    own_x.wait_recv()
    own_y.wait_recv()
    for i in range(2):
        for side in range(2):
            (last_x if side else last_y)[i].wait_recv()
            finish(side, i)
            for step in range(1, n_z):
                deliver(side, i, step).start()
    for i in range(2):
        for side in range(2):
            collect(side, i)

    for copy in [own_x, own_y] + pass_x + pass_y + last_x + last_y:
        copy.wait_send()
    for part in range(2):
        proj_pair(part).wait_send()
        proj_x(part).wait_send()
    for slot, q in enumerate((q_own, q_x, q_y, q_d)):
        for block in range(n_z):
            share(q, c, slot, block).wait_send()
        for part in range(2):
            pair(q, slot, part).wait_send()
    for step in range(1, n_z):
        for i in range(2):
            for side in range(2):
                deliver(side, i, step).wait_send()
    for block in range(n_z):
        keys_y(block, y).wait_send()
        pl.when((z + 1 < n_z) & (block <= z))(lambda: keys_z(block, True).wait_send())
        pl.when((z >= 1) & (block >= z))(lambda: keys_z(block, False).wait_send())
        over_x(q_own, block).wait_send()
        over_y(q_own, block).wait_send()
        diag_x(q_y, block).wait_send()
        diag_y(q_x, block).wait_send()
        pl.when((z + 1 < n_z) & (block <= z))(lambda: along_z(block, True).wait_send())
        pl.when((z >= 1) & (block >= z))(lambda: along_z(block, False).wait_send())


def whole_layer(
    queries,
    keys_values,
    residual,
    norm_gain,
    w_out,
    w_gate_up,
    w_down,
    expert_ids,
    mix_weights,
    clip_lengths,
):
    n_ep = lax.axis_size("ep")
    n_z = n_ep // 2
    n_experts = n_ep * lax.axis_size("tp")
    rows, half = residual.shape
    q_rows = queries.shape[0]
    parts = 3
    width = half + -(-parts * n_experts // 128) * 128
    many = n_z * rows
    cut = half // 2
    dma = pltpu.SemaphoreType.DMA
    bf16 = jnp.bfloat16
    in_vmem = pl.BlockSpec(memory_space=pltpu.VMEM)
    return pl.pallas_call(
        functools.partial(layer_kernel, n_z, n_experts, parts),
        out_shape=jax.ShapeDtypeStruct((rows, half), bf16),
        in_specs=[pl.BlockSpec(memory_space=pltpu.SMEM)]
        + [pl.BlockSpec(memory_space=pltpu.HBM)] * 9,
        out_specs=in_vmem,
        scratch_shapes=[
            pltpu.VMEM(queries.shape, bf16),
            pltpu.VMEM(residual.shape, bf16),
            pltpu.VMEM((1, half), jnp.float32),
            pltpu.VMEM(expert_ids.shape[::-1], jnp.int32),
            pltpu.VMEM(mix_weights.shape[::-1], jnp.float32),
            pltpu.VMEM((n_ep, q_rows, 2 * HD), bf16),
            pltpu.VMEM(queries.shape, bf16),
            pltpu.VMEM((2, 2, rows, half), bf16),
            pltpu.VMEM((2, rows, half), bf16),
            pltpu.VMEM((rows, half), bf16),
            pltpu.VMEM((rows, half), jnp.float32),
            pltpu.VMEM(w_out.shape, bf16),
            dma((2, n_z)),
            dma((n_z,)),
            dma((n_z,)),
            dma((n_z,)),
            dma((4,)),
            dma((4,)),
            pltpu.VMEM((4, 2, n_z, rows, width), bf16),
            pltpu.VMEM(w_gate_up.shape[1:], bf16),
            pltpu.VMEM(w_down.shape[1:], bf16),
            pltpu.VMEM((4, 2, many, half), bf16),
            pltpu.VMEM((4, many, half), bf16),
            pltpu.VMEM((many, cut), bf16),
            pltpu.VMEM((many, cut), bf16),
            pltpu.VMEM((2, many, cut), bf16),
            pltpu.VMEM((2, many, cut), bf16),
            pltpu.VMEM((2, 2, n_z - 1, rows, cut // 2), bf16),
            dma((9,)),
            dma((2, n_z)),
        ]
        + [dma((n_z,))] * 9
        + [dma((4, n_z))] * 2
        + [dma((4, 2))] * 2
        + [dma((10,))] * 2
        + [dma((2, 2, n_z - 1))] * 2,
        compiler_params=pltpu.CompilerParams(
            collective_id=0, has_side_effects=True, vmem_limit_bytes=62 * 1024 * 1024
        ),
    )(
        clip_lengths,
        queries,
        keys_values,
        residual,
        norm_gain.reshape(1, half),
        expert_ids.T,
        mix_weights.T,
        w_out,
        w_gate_up,
        w_down,
    )


def body(
    queries,
    keys_values,
    residual,
    norm_gain,
    w_out,
    w_gate_up,
    w_down,
    expert_ids,
    mix_weights,
    clip_lengths,
):
    rows = queries.shape[0]
    heads_here = queries.shape[1] // HD
    if (
        lax.axis_size("pool") == 1
        and lax.axis_size("tp") == 4
        and lax.axis_size("ep") % 2 == 0
        and lax.axis_size("ep") > 2
        and heads_here == QH // KVH
        and w_gate_up.shape[0] == 1
        and residual.shape[0] % 16 == 0
        and residual.shape[1] == D
        and rows == 4 * residual.shape[0]
    ):
        return whole_layer(
            queries,
            keys_values,
            residual,
            norm_gain,
            w_out,
            w_gate_up,
            w_down,
            expert_ids,
            mix_weights,
            clip_lengths,
        )
    pool_size = lax.axis_size("pool")
    tensor_size = lax.axis_size("tp")
    context_size = lax.axis_size("ep")
    pool_index = lax.axis_index("pool")
    tensor_index = lax.axis_index("tp")
    pair_heads = keys_values.shape[1] // (2 * HD)
    group = QH // KVH
    head_pick = (
        pool_index * tensor_size + tensor_index
    ) * heads_here // group - pool_index * pair_heads
    own_pairs = lax.dynamic_slice_in_dim(keys_values, head_pick * (2 * HD), 2 * HD, 1)
    places = lax.axis_index("ep") * rows + jnp.arange(rows, dtype=jnp.int32)
    query_clip = clip_index(clip_lengths, places)
    query_heads = queries.reshape(rows, heads_here, HD)
    scale = HD ** (-0.5)
    start_state = (
        jnp.full((heads_here, rows), -1e30, jnp.float32),
        jnp.zeros((heads_here, rows), jnp.float32),
        jnp.zeros((heads_here, rows, HD), jnp.float32),
    )
    piece = lax.all_gather(own_pairs, "ep", axis=0, tiled=True)
    length = piece.shape[0]
    stride = min(length, rows * max(1, 512 // rows))
    while length % stride:
        stride = stride - 1

    def one_block(index, state):
        top, total, numer = state
        block = lax.dynamic_slice_in_dim(piece, index * stride, stride, 0)
        key_clip = clip_index(clip_lengths, index * stride + jnp.arange(stride, dtype=jnp.int32))
        scores = (
            jnp.einsum(
                "rhd,nd->hrn", query_heads, block[:, :HD], preferred_element_type=jnp.float32
            )
            * scale
        )
        same = (query_clip[:, None] == key_clip[None, :])[None, :, :]
        new_top = jnp.maximum(top, jnp.max(jnp.where(same, scores, -1e30), axis=2))
        weights = jnp.where(same, jnp.exp(scores - new_top[:, :, None]), 0.0)
        factor = jnp.exp(top - new_top)
        total = total * factor + jnp.sum(weights, axis=2)
        numer = numer * factor[:, :, None] + jnp.einsum(
            "hrn,nd->hrd",
            weights.astype(jnp.bfloat16),
            block[:, HD:],
            preferred_element_type=jnp.float32,
        )
        return (new_top, total, numer)

    top, total, numer = lax.fori_loop(0, length // stride, one_block, start_state)
    attended = (numer / total[:, :, None]).astype(jnp.bfloat16)
    half = residual.shape[1]
    out_heads = w_out.reshape(heads_here, HD, pool_size * half)
    moe_rows = residual.shape[0]
    start = jnp.int32(0)
    pieces = []
    for offset in range(lax.axis_size(("pool", "tp")) * moe_rows // rows):
        part = start // rows + offset
        weights = lax.dynamic_slice_in_dim(out_heads, part * half, half, 2)
        pieces.append(
            jnp.einsum("hrd,hde->re", attended, weights, preferred_element_type=jnp.float32)
        )
    mixed = lax.psum_scatter(
        jnp.concatenate(pieces, axis=0).astype(jnp.bfloat16),
        ("pool", "tp"),
        scatter_dimension=0,
        tiled=True,
    ).astype(jnp.float32)
    hidden_state = residual.astype(jnp.float32) + mixed
    squares = lax.psum(jnp.sum(hidden_state * hidden_state, axis=1), "pool")
    normed = (hidden_state * lax.rsqrt(squares / D + 1e-06)[:, None] * norm_gain[None, :]).astype(
        jnp.bfloat16
    )
    top_k = expert_ids.shape[1]
    local_experts = w_gate_up.shape[0]
    experts = local_experts * context_size * tensor_size
    capacity = 2 * moe_rows * top_k // experts
    flat = expert_ids.reshape(-1)
    marks = (flat[:, None] == jnp.arange(experts, dtype=jnp.int32)[None, :]).astype(jnp.int32)
    rank = jnp.sum(jnp.cumsum(marks, axis=0) * marks, axis=1) - 1
    slot = flat * capacity + rank
    source = jnp.arange(moe_rows * top_k, dtype=jnp.int32) // top_k
    outgoing = jnp.zeros((experts * capacity, half), jnp.bfloat16).at[slot].set(normed[source])
    hidden_width = w_down.shape[1]
    shaped = outgoing.reshape(experts, capacity, half)
    arrived = lax.all_to_all(shaped, ("ep", "tp"), split_axis=0, concat_axis=0, tiled=True)
    width = arrived.shape[1]
    grouped = arrived.reshape(-1, local_experts, width, half)
    both = jnp.einsum("slcd,ldf->slcf", grouped, w_gate_up, preferred_element_type=jnp.float32)
    both = lax.psum(both.astype(jnp.bfloat16), "pool").astype(jnp.float32)
    hidden = (jax.nn.silu(both[..., :hidden_width]) * both[..., hidden_width:]).astype(jnp.bfloat16)
    result = jnp.einsum(
        "slcf,lfd->slcd", hidden, w_down, preferred_element_type=jnp.float32
    ).astype(jnp.bfloat16)
    finished = result.reshape(-1, width, half)
    back = lax.all_to_all(finished, ("ep", "tp"), split_axis=0, concat_axis=0, tiled=True)
    back_rows = back.reshape(experts * capacity, half)[slot]
    gathered = back_rows.reshape(moe_rows, top_k, half).astype(jnp.float32)
    blended = jnp.sum(gathered * mix_weights[:, :, None], axis=1)
    return (hidden_state + blended).astype(jnp.bfloat16)


def solution(mesh):
    placed = (
        P(("grp", "ep"), ("pool", "tp")),
        P(("grp", "ep"), "pool"),
        P(("grp", "ep", "tp"), "pool"),
        P("pool"),
        P(("pool", "tp"), None),
        P(("ep", "tp"), "pool", None),
        P(("ep", "tp"), None, "pool"),
        P(("grp", "ep", "tp"), None),
        P(("grp", "ep", "tp"), None),
        P("grp"),
    )
    return jax.shard_map(
        body, mesh=mesh, in_specs=placed, out_specs=P(("grp", "ep", "tp"), "pool"), check_vma=False
    )
```

```python
import functools
import math

import jax
import jax.numpy as jnp
from jax import lax
from jax.experimental import pallas as pl
from jax.experimental.pallas import tpu as pltpu
from jax.sharding import PartitionSpec as P

D = 2048
QH = 32
KVH = 4
HD = 128


def clip_index(clip_lengths, places):
    ends = jnp.cumsum(clip_lengths)
    return jnp.sum((places[:, None] >= ends[None, :]).astype(jnp.int32), axis=1)


def layer_kernel(
    n_z,
    n_experts,
    parts,
    clip_hbm,
    queries_hbm,
    kv_hbm,
    residual_hbm,
    gain_hbm,
    ids_hbm,
    mix_hbm,
    wo_hbm,
    wgu_hbm,
    wd_hbm,
    out_ref,
    clip_ref,
    queries_ref,
    residual_ref,
    gain_ref,
    ids_ref,
    mix_ref,
    kv,
    attended,
    proj,
    sib_in,
    x_in,
    hidden_ref,
    wo,
    kz_send,
    kz_recv,
    ky_send,
    ky_recv,
    at_send,
    at_recv,
    held,
    wgu,
    wd,
    term,
    pair_in,
    relay_x,
    relay_y,
    from_x,
    from_y,
    from_z,
    w_sem,
    z_send,
    z_recv,
    x_send,
    x_recv,
    y_send,
    y_recv,
    da_send,
    da_recv,
    db_send,
    db_recv,
    sib_send,
    sib_recv,
    pair_send,
    pair_recv,
    r_send,
    r_recv,
    rz_send,
    rz_recv,
):
    ep = lax.axis_index("ep")
    tp = lax.axis_index("tp")
    z, y = ep // 2, ep % 2
    x, c = tp // 2, tp % 2
    rows, half = residual_ref.shape
    cut = half // 2
    quarter = half // 4
    width = held.shape[4]
    q_rows = queries_ref.shape[0]
    first, second, rest = pl.ds(0, cut), pl.ds(cut, cut), pl.ds(cut, width - cut)
    x_peer = (ep, (1 - x) * 2 + c)
    y_peer = (z * 2 + 1 - y, tp)
    sib = (ep, x * 2 + 1 - c)
    q_own, q_x = x * 2 + y, (1 - x) * 2 + y
    q_y, q_d = x * 2 + 1 - y, (1 - x) * 2 + 1 - y

    pair_width = kv.shape[2]
    own_keys = kv_hbm.at[:, pl.ds(pl.multiple_of(tp * pair_width, pair_width), pair_width)]
    loads = [
        pltpu.make_async_copy(src, dst, w_sem.at[number])
        for number, (src, dst) in enumerate(
            (
                (own_keys, kv.at[ep]),
                (queries_hbm, queries_ref),
                (ids_hbm, ids_ref),
                (mix_hbm, mix_ref),
                (residual_hbm, residual_ref),
                (gain_hbm, gain_ref),
                (wo_hbm, wo),
                (wgu_hbm.at[0], wgu),
                (wd_hbm.at[0], wd),
                (clip_hbm, clip_ref),
            )
        )
    ]
    for load in loads:
        load.start()

    barrier = pltpu.get_barrier_semaphore()
    for peer in (x_peer, y_peer, sib):
        pl.semaphore_signal(
            barrier,
            inc=1,
            device_id={"ep": peer[0], "tp": peer[1]},
            device_id_type=pl.DeviceIdType.MESH,
        )
    for step in range(1, n_z):
        pl.semaphore_signal(
            barrier,
            inc=1,
            device_id={"ep": ((z + step) % n_z) * 2 + y, "tp": tp},
            device_id_type=pl.DeviceIdType.MESH,
        )

    def remote(src, dst, send, recv, peer):
        return pltpu.make_async_remote_copy(
            src_ref=src,
            dst_ref=dst,
            send_sem=send,
            recv_sem=recv,
            device_id={"ep": peer[0], "tp": peer[1]},
            device_id_type=pl.DeviceIdType.MESH,
        )

    def along_z(block, up):
        there = z + 1 if up else z - 1
        return remote(
            held.at[q_own, c, block],
            held.at[q_own, c, block],
            z_send.at[1 if up else 0, block],
            z_recv.at[block],
            (there * 2 + y, tp),
        )

    def over_x(q, block):
        here = held.at[q, c, block]
        return remote(here, here, x_send.at[block], x_recv.at[block], x_peer)

    def over_y(q, block):
        here = held.at[q, c, block]
        return remote(here, here, y_send.at[block], y_recv.at[block], y_peer)

    def diag_x(q, block):
        here = held.at[q, c, block, :, first]
        return remote(here, here, da_send.at[block], da_recv.at[block], x_peer)

    def diag_y(q, block):
        here = held.at[q, c, block, :, rest]
        return remote(here, here, db_send.at[block], db_recv.at[block], y_peer)

    def share(q, core, slot, block):
        here = held.at[q, core, block]
        return remote(here, here, sib_send.at[slot, block], sib_recv.at[slot, block], sib)

    def shares_arrive(q, slot):
        for block in range(n_z):
            share(q, 1 - c, slot, block).wait_recv()

    def each_at(distance, act):
        if distance == 0:
            act(z, 0)
            return
        pl.when(z - distance >= 0)(lambda: act(z - distance, -1))
        pl.when(z + distance < n_z)(lambda: act(z + distance, 1))

    def keys_z(block, up):
        there = z + 1 if up else z - 1
        here = kv.at[block * 2 + y]
        return remote(
            here, here, kz_send.at[1 if up else 0, block], kz_recv.at[block], (there * 2 + y, tp)
        )

    def keys_y(block, side_y):
        here = kv.at[block * 2 + side_y]
        return remote(here, here, ky_send.at[block], ky_recv.at[block], y_peer)

    def keys_arrive(block, side):
        if side:
            keys_z(block, side < 0).wait_recv()
        if side <= 0:
            pl.when(z + 1 < n_z)(lambda: keys_z(block, True).start())
        if side >= 0:
            pl.when(z >= 1)(lambda: keys_z(block, False).start())
        keys_y(block, y).start()

    head = pair_width // 2
    loads[0].wait()
    pl.semaphore_wait(barrier, 3 + n_z - 1)
    for distance in range(n_z):
        each_at(distance, keys_arrive)

    n_keys = 2 * n_z * q_rows
    place = lax.broadcasted_iota(jnp.int32, (2 * q_rows, 1), 0)
    place = jnp.where(place >= q_rows, place - q_rows, place) + ep * q_rows
    key_place = lax.broadcasted_iota(jnp.int32, (1, n_keys), 1)
    clip = jnp.zeros(place.shape, jnp.int32)
    key_clip = jnp.zeros(key_place.shape, jnp.int32)
    end = jnp.int32(0)
    loads[9].wait()
    for number in range(clip_ref.shape[0]):
        end = end + clip_ref[number]
        clip = clip + jnp.where(place >= end, 1, 0)
        key_clip = key_clip + jnp.where(key_place >= end, 1, 0)
    same = clip == key_clip

    loads[2].wait()
    loads[3].wait()
    lane = lax.broadcasted_iota(jnp.int32, (width - half, rows), 0)
    base = jnp.zeros(lane.shape, jnp.int32)
    for part in range(1, parts):
        base = base + jnp.where(lane >= part * n_experts, n_experts, 0)
    wanted = lane - base
    weight = jnp.zeros(lane.shape, jnp.float32)
    for slot in range(ids_ref.shape[0]):
        weight = weight + jnp.where(
            ids_ref[slot : slot + 1, :] == wanted, mix_ref[slot : slot + 1, :], 0.0
        )
    packed = jnp.zeros(lane.shape, jnp.float32)
    for part in range(parts):
        piece = weight.astype(jnp.bfloat16).astype(jnp.float32)
        packed = jnp.where(base == part * n_experts, piece, packed)
        weight = weight - piece
    unit = lax.broadcasted_iota(jnp.int32, (rows, rows), 0) == lax.broadcasted_iota(
        jnp.int32, (rows, rows), 1
    )
    held[q_own, c, z, :, half:width] = lax.dot_general(
        jnp.where(unit, 1.0, 0.0).astype(jnp.bfloat16),
        packed.astype(jnp.bfloat16),
        (((1,), (1,)), ((), ())),
        preferred_element_type=jnp.float32,
    ).astype(jnp.bfloat16)

    loads[1].wait()
    for block in range(n_z):
        keys_y(block, 1 - y).wait_recv()
    keys = kv[:, :, 0:head].reshape(n_keys, head)
    values = kv[:, :, head:pair_width].reshape(n_keys, head)
    scale = head ** (-0.5) * math.log2(math.e)
    for at in range(0, queries_ref.shape[1], 2 * head):
        two = jnp.concatenate(
            [queries_ref[:, at : at + head], queries_ref[:, at + head : at + 2 * head]], axis=0
        )
        scores = lax.dot_general(
            two, keys, (((1,), (1,)), ((), ())), preferred_element_type=jnp.float32
        )
        scores = jnp.where(same, scores, -1e30)
        top = jnp.max(scores, axis=1, keepdims=True)
        weights = jnp.exp2((scores - top) * scale)
        total = jnp.sum(weights, axis=1, keepdims=True)
        numer = jnp.dot(
            weights.astype(jnp.bfloat16), values, preferred_element_type=jnp.float32
        )
        result = (numer / total).astype(jnp.bfloat16)
        attended[:, at : at + head] = result[0:q_rows]
        attended[:, at + head : at + 2 * head] = result[q_rows : 2 * q_rows]

    def proj_pair(part):
        columns = pl.ds(part * cut, cut)
        return remote(
            proj.at[1 - c, :, :, columns],
            sib_in.at[:, :, columns],
            at_send.at[part],
            at_recv.at[part],
            sib,
        )

    def proj_x(part):
        columns = pl.ds(part * cut, cut)
        return remote(
            proj.at[c, 1 - x, :, columns],
            x_in.at[:, columns],
            at_send.at[2 + part],
            at_recv.at[2 + part],
            x_peer,
        )

    loads[6].wait()
    for part in range(2):
        for at in range(part * cut, (part + 1) * cut, quarter):
            result = jnp.dot(
                attended[...], wo[:, at : at + quarter], preferred_element_type=jnp.float32
            ).astype(jnp.bfloat16)
            for side_x in range(2):
                for side_c in range(2):
                    start = (side_x * 2 + side_c) * rows
                    proj[side_c, side_x, :, at : at + quarter] = result[start : start + rows]
        proj_pair(part).start()
    for part in range(2):
        columns = pl.ds(part * cut, cut)
        proj_pair(part).wait_recv()
        proj[c, 1 - x, :, columns] = (
            proj[c, 1 - x, :, columns].astype(jnp.float32)
            + sib_in[1 - x, :, columns].astype(jnp.float32)
        ).astype(jnp.bfloat16)
        proj_x(part).start()
    loads[4].wait()
    loads[5].wait()
    for part in range(2):
        columns = pl.ds(part * cut, cut)
        hidden_ref[:, columns] = (
            residual_ref[:, columns].astype(jnp.float32)
            + proj[c, x, :, columns].astype(jnp.float32)
            + sib_in[x, :, columns].astype(jnp.float32)
        )
    for part in range(2):
        columns = pl.ds(part * cut, cut)
        proj_x(part).wait_recv()
        hidden_ref[:, columns] += x_in[:, columns].astype(jnp.float32)
    hidden = hidden_ref[...]
    squares = jnp.sum(hidden * hidden, axis=1, keepdims=True) / half
    held[q_own, c, z, :, 0:half] = (hidden * lax.rsqrt(squares + 1e-06) * gain_ref[...]).astype(
        jnp.bfloat16
    )

    def arrive_z(block, side):
        if side:
            along_z(block, side < 0).wait_recv()
        if side <= 0:
            pl.when(z + 1 < n_z)(lambda: along_z(block, True).start())
        if side >= 0:
            pl.when(z >= 1)(lambda: along_z(block, False).start())
        over_x(q_own, block).start()
        over_y(q_own, block).start()
        share(q_own, c, 0, block).start()

    def arrive_xy(block, side):
        over_x(q_x, block).wait_recv()
        diag_y(q_x, block).start()
        share(q_x, c, 1, block).start()
        over_y(q_y, block).wait_recv()
        diag_x(q_y, block).start()
        share(q_y, c, 2, block).start()

    def arrive_diag(block, side):
        diag_x(q_d, block).wait_recv()
        diag_y(q_d, block).wait_recv()
        share(q_d, c, 3, block).start()

    mine = ep * lax.axis_size("tp") + tp
    many = 2 * n_z * rows

    def pair(q, slot, part):
        columns = pl.ds(part * cut, cut)
        return remote(
            term.at[q, 1 - c, :, columns],
            pair_in.at[slot, :, columns],
            pair_send.at[slot, part],
            pair_recv.at[slot, part],
            sib,
        )

    def compute(q, slot):
        both = jnp.dot(
            held[q, :, :, :, 0:half].reshape(many, half),
            wgu[...],
            preferred_element_type=jnp.float32,
        )
        ff = both.shape[1] // 2
        gate, up = both[:, :ff], both[:, ff:]
        acted = (gate / (1.0 + jnp.exp(-gate)) * up).astype(jnp.bfloat16)
        shares = held[q, :, :, :, half:width].reshape(many, width - half).astype(jnp.float32)
        lane = lax.broadcasted_iota(jnp.int32, shares.shape, 1)
        wanted = lane == mine
        for part in range(1, parts):
            wanted = wanted | (lane == mine + part * n_experts)
        mix = jnp.sum(jnp.where(wanted, shares, 0.0), axis=1, keepdims=True)
        tile = half // 4
        for at in range(0, half, tile):
            result = jnp.dot(
                acted, wd[:, at : at + tile], preferred_element_type=jnp.float32
            ).astype(jnp.bfloat16)
            term[q, :, :, at : at + tile] = (
                (result.astype(jnp.float32) * mix)
                .astype(jnp.bfloat16)
                .reshape(2, n_z * rows, tile)
            )
            if (at + tile) % cut == 0:
                pair(q, slot, at // cut).start()

    def add_pair(q, slot, part):
        pair(q, slot, part).wait_recv()
        to = pl.ds(part * cut, cut)
        term[q, c, :, to] = (
            term[q, c, :, to].astype(jnp.float32) + pair_in[slot, :, to].astype(jnp.float32)
        ).astype(jnp.bfloat16)

    def reduce_x(q, columns, into, slot):
        return remote(term.at[q, c, :, columns], into, r_send.at[slot], r_recv.at[slot], x_peer)

    def reduce_y(q, columns, into, slot):
        return remote(term.at[q, c, :, columns], into, r_send.at[slot], r_recv.at[slot], y_peer)

    chunks = from_z.shape[1]
    piece_width = cut // chunks
    low = [pl.ds(i * piece_width, piece_width) for i in range(chunks)]
    high = [pl.ds(cut + i * piece_width, piece_width) for i in range(chunks)]
    own_x = reduce_x(q_x, first, from_x.at[0], 0)
    own_y = reduce_y(q_y, second, from_y.at[1], 1)
    pass_x = [reduce_x(q_d, low[i], relay_x.at[:, low[i]], 2 + i) for i in range(chunks)]
    pass_y = [reduce_y(q_d, high[i], relay_y.at[:, low[i]], 6 + i) for i in range(chunks)]
    last_x = [reduce_x(q_x, high[i], from_x.at[1, :, low[i]], 10 + i) for i in range(chunks)]
    last_y = [reduce_y(q_y, low[i], from_y.at[0, :, low[i]], 14 + i) for i in range(chunks)]

    for distance in range(n_z):
        each_at(distance, arrive_z)
        if distance >= 1:
            each_at(distance - 1, arrive_xy)
    loads[7].wait()
    loads[8].wait()
    shares_arrive(q_own, 0)
    compute(q_own, 0)
    each_at(n_z - 1, arrive_xy)
    shares_arrive(q_x, 1)
    compute(q_x, 1)
    for distance in range(n_z - 2):
        each_at(distance, arrive_diag)
    shares_arrive(q_y, 2)
    add_pair(q_x, 1, 0)
    own_x.start()
    compute(q_y, 2)
    for distance in range(max(n_z - 2, 0), n_z):
        each_at(distance, arrive_diag)
    add_pair(q_y, 2, 1)
    own_y.start()
    shares_arrive(q_d, 3)
    compute(q_d, 3)
    add_pair(q_d, 3, 0)
    for copy in pass_x[:2]:
        copy.start()
    add_pair(q_d, 3, 1)
    for copy in pass_y[:2]:
        copy.start()
    add_pair(q_y, 2, 0)
    add_pair(q_x, 1, 1)
    add_pair(q_own, 0, 0)
    add_pair(q_own, 0, 1)

    def relay(i):
        pass_x[i].wait_recv()
        term[q_y, c, :, low[i]] = (
            term[q_y, c, :, low[i]].astype(jnp.float32) + relay_x[:, low[i]].astype(jnp.float32)
        ).astype(jnp.bfloat16)
        last_y[i].start()
        pass_y[i].wait_recv()
        term[q_x, c, :, high[i]] = (
            term[q_x, c, :, high[i]].astype(jnp.float32) + relay_y[:, low[i]].astype(jnp.float32)
        ).astype(jnp.bfloat16)
        last_x[i].start()
        if i + 2 < chunks:
            pass_x[i + 2].start()
            pass_y[i + 2].start()

    def finish(side, i):
        columns = high[i] if side else low[i]
        term[q_own, c, :, columns] = (
            term[q_own, c, :, columns].astype(jnp.float32)
            + from_x[side, :, low[i]].astype(jnp.float32)
            + from_y[side, :, low[i]].astype(jnp.float32)
        ).astype(jnp.bfloat16)

    def deliver(side, i, step):
        there = (z + step) % n_z
        return remote(
            term.at[
                q_own,
                c,
                pl.ds(pl.multiple_of(there * rows, rows), rows),
                high[i] if side else low[i],
            ],
            from_z.at[side, i, n_z - 1 - step],
            rz_send.at[side, i, step - 1],
            rz_recv.at[side, i, n_z - 1 - step],
            (there * 2 + y, tp),
        )

    def collect(side, i):
        columns = high[i] if side else low[i]
        total = hidden_ref[:, columns] + term[
            q_own, c, pl.ds(pl.multiple_of(z * rows, rows), rows), columns
        ].astype(jnp.float32)
        for step in range(1, n_z):
            deliver(side, i, step).wait_recv()
            total = total + from_z[side, i, n_z - 1 - step].astype(jnp.float32)
        out_ref[:, columns] = total.astype(jnp.bfloat16)

    def complete(i):
        for side in range(2):
            (last_x if side else last_y)[i].wait_recv()
            finish(side, i)
            for step in range(1, n_z):
                deliver(side, i, step).start()

    relay(0)
    own_x.wait_recv()
    own_y.wait_recv()
    for i in range(1, chunks):
        relay(i)
        complete(i - 1)
    complete(chunks - 1)
    for i in range(chunks):
        for side in range(2):
            collect(side, i)

    for copy in [own_x, own_y] + pass_x + pass_y + last_x + last_y:
        copy.wait_send()
    for part in range(2):
        proj_pair(part).wait_send()
        proj_x(part).wait_send()
    for slot, q in enumerate((q_own, q_x, q_y, q_d)):
        for block in range(n_z):
            share(q, c, slot, block).wait_send()
        for part in range(2):
            pair(q, slot, part).wait_send()
    for step in range(1, n_z):
        for i in range(chunks):
            for side in range(2):
                deliver(side, i, step).wait_send()
    for block in range(n_z):
        keys_y(block, y).wait_send()
        pl.when((z + 1 < n_z) & (block <= z))(lambda: keys_z(block, True).wait_send())
        pl.when((z >= 1) & (block >= z))(lambda: keys_z(block, False).wait_send())
        over_x(q_own, block).wait_send()
        over_y(q_own, block).wait_send()
        diag_x(q_y, block).wait_send()
        diag_y(q_x, block).wait_send()
        pl.when((z + 1 < n_z) & (block <= z))(lambda: along_z(block, True).wait_send())
        pl.when((z >= 1) & (block >= z))(lambda: along_z(block, False).wait_send())


def whole_layer(
    queries,
    keys_values,
    residual,
    norm_gain,
    w_out,
    w_gate_up,
    w_down,
    expert_ids,
    mix_weights,
    clip_lengths,
):
    n_ep = lax.axis_size("ep")
    n_z = n_ep // 2
    n_experts = n_ep * lax.axis_size("tp")
    rows, half = residual.shape
    q_rows = queries.shape[0]
    parts = 3
    width = half + -(-parts * n_experts // 128) * 128
    many = n_z * rows
    cut = half // 2
    chunks = 4
    dma = pltpu.SemaphoreType.DMA
    bf16 = jnp.bfloat16
    in_vmem = pl.BlockSpec(memory_space=pltpu.VMEM)
    return pl.pallas_call(
        functools.partial(layer_kernel, n_z, n_experts, parts),
        out_shape=jax.ShapeDtypeStruct((rows, half), bf16),
        in_specs=[pl.BlockSpec(memory_space=pltpu.HBM)] * 10,
        out_specs=in_vmem,
        scratch_shapes=[
            pltpu.SMEM(clip_lengths.shape, jnp.int32),
            pltpu.VMEM(queries.shape, bf16),
            pltpu.VMEM(residual.shape, bf16),
            pltpu.VMEM((1, half), jnp.float32),
            pltpu.VMEM(expert_ids.shape[::-1], jnp.int32),
            pltpu.VMEM(mix_weights.shape[::-1], jnp.float32),
            pltpu.VMEM((n_ep, q_rows, 2 * HD), bf16),
            pltpu.VMEM(queries.shape, bf16),
            pltpu.VMEM((2, 2, rows, half), bf16),
            pltpu.VMEM((2, rows, half), bf16),
            pltpu.VMEM((rows, half), bf16),
            pltpu.VMEM((rows, half), jnp.float32),
            pltpu.VMEM(w_out.shape, bf16),
            dma((2, n_z)),
            dma((n_z,)),
            dma((n_z,)),
            dma((n_z,)),
            dma((4,)),
            dma((4,)),
            pltpu.VMEM((4, 2, n_z, rows, width), bf16),
            pltpu.VMEM(w_gate_up.shape[1:], bf16),
            pltpu.VMEM(w_down.shape[1:], bf16),
            pltpu.VMEM((4, 2, many, half), bf16),
            pltpu.VMEM((4, many, half), bf16),
            pltpu.VMEM((many, cut), bf16),
            pltpu.VMEM((many, cut), bf16),
            pltpu.VMEM((2, many, cut), bf16),
            pltpu.VMEM((2, many, cut), bf16),
            pltpu.VMEM((2, chunks, n_z - 1, rows, cut // chunks), bf16),
            dma((10,)),
            dma((2, n_z)),
        ]
        + [dma((n_z,))] * 9
        + [dma((4, n_z))] * 2
        + [dma((4, 2))] * 2
        + [dma((2 + 4 * chunks,))] * 2
        + [dma((2, chunks, n_z - 1))] * 2,
        compiler_params=pltpu.CompilerParams(
            collective_id=0, has_side_effects=True, vmem_limit_bytes=62 * 1024 * 1024
        ),
    )(
        clip_lengths,
        queries,
        keys_values,
        residual,
        norm_gain.reshape(1, half),
        expert_ids.T,
        mix_weights.T,
        w_out,
        w_gate_up,
        w_down,
    )


def body(
    queries,
    keys_values,
    residual,
    norm_gain,
    w_out,
    w_gate_up,
    w_down,
    expert_ids,
    mix_weights,
    clip_lengths,
):
    rows = queries.shape[0]
    heads_here = queries.shape[1] // HD
    if (
        lax.axis_size("pool") == 1
        and lax.axis_size("tp") == 4
        and lax.axis_size("ep") % 2 == 0
        and lax.axis_size("ep") > 2
        and heads_here == QH // KVH
        and w_gate_up.shape[0] == 1
        and residual.shape[0] % 16 == 0
        and residual.shape[1] == D
        and rows == 4 * residual.shape[0]
    ):
        return whole_layer(
            queries,
            keys_values,
            residual,
            norm_gain,
            w_out,
            w_gate_up,
            w_down,
            expert_ids,
            mix_weights,
            clip_lengths,
        )
    pool_size = lax.axis_size("pool")
    tensor_size = lax.axis_size("tp")
    context_size = lax.axis_size("ep")
    pool_index = lax.axis_index("pool")
    tensor_index = lax.axis_index("tp")
    pair_heads = keys_values.shape[1] // (2 * HD)
    group = QH // KVH
    head_pick = (
        pool_index * tensor_size + tensor_index
    ) * heads_here // group - pool_index * pair_heads
    own_pairs = lax.dynamic_slice_in_dim(keys_values, head_pick * (2 * HD), 2 * HD, 1)
    places = lax.axis_index("ep") * rows + jnp.arange(rows, dtype=jnp.int32)
    query_clip = clip_index(clip_lengths, places)
    query_heads = queries.reshape(rows, heads_here, HD)
    scale = HD ** (-0.5)
    start_state = (
        jnp.full((heads_here, rows), -1e30, jnp.float32),
        jnp.zeros((heads_here, rows), jnp.float32),
        jnp.zeros((heads_here, rows, HD), jnp.float32),
    )
    piece = lax.all_gather(own_pairs, "ep", axis=0, tiled=True)
    length = piece.shape[0]
    stride = min(length, rows * max(1, 512 // rows))
    while length % stride:
        stride = stride - 1

    def one_block(index, state):
        top, total, numer = state
        block = lax.dynamic_slice_in_dim(piece, index * stride, stride, 0)
        key_clip = clip_index(clip_lengths, index * stride + jnp.arange(stride, dtype=jnp.int32))
        scores = (
            jnp.einsum(
                "rhd,nd->hrn", query_heads, block[:, :HD], preferred_element_type=jnp.float32
            )
            * scale
        )
        same = (query_clip[:, None] == key_clip[None, :])[None, :, :]
        new_top = jnp.maximum(top, jnp.max(jnp.where(same, scores, -1e30), axis=2))
        weights = jnp.where(same, jnp.exp(scores - new_top[:, :, None]), 0.0)
        factor = jnp.exp(top - new_top)
        total = total * factor + jnp.sum(weights, axis=2)
        numer = numer * factor[:, :, None] + jnp.einsum(
            "hrn,nd->hrd",
            weights.astype(jnp.bfloat16),
            block[:, HD:],
            preferred_element_type=jnp.float32,
        )
        return (new_top, total, numer)

    top, total, numer = lax.fori_loop(0, length // stride, one_block, start_state)
    attended = (numer / total[:, :, None]).astype(jnp.bfloat16)
    half = residual.shape[1]
    out_heads = w_out.reshape(heads_here, HD, pool_size * half)
    moe_rows = residual.shape[0]
    start = jnp.int32(0)
    pieces = []
    for offset in range(lax.axis_size(("pool", "tp")) * moe_rows // rows):
        part = start // rows + offset
        weights = lax.dynamic_slice_in_dim(out_heads, part * half, half, 2)
        pieces.append(
            jnp.einsum("hrd,hde->re", attended, weights, preferred_element_type=jnp.float32)
        )
    mixed = lax.psum_scatter(
        jnp.concatenate(pieces, axis=0).astype(jnp.bfloat16),
        ("pool", "tp"),
        scatter_dimension=0,
        tiled=True,
    ).astype(jnp.float32)
    hidden_state = residual.astype(jnp.float32) + mixed
    squares = lax.psum(jnp.sum(hidden_state * hidden_state, axis=1), "pool")
    normed = (hidden_state * lax.rsqrt(squares / D + 1e-06)[:, None] * norm_gain[None, :]).astype(
        jnp.bfloat16
    )
    top_k = expert_ids.shape[1]
    local_experts = w_gate_up.shape[0]
    experts = local_experts * context_size * tensor_size
    capacity = 2 * moe_rows * top_k // experts
    flat = expert_ids.reshape(-1)
    marks = (flat[:, None] == jnp.arange(experts, dtype=jnp.int32)[None, :]).astype(jnp.int32)
    rank = jnp.sum(jnp.cumsum(marks, axis=0) * marks, axis=1) - 1
    slot = flat * capacity + rank
    source = jnp.arange(moe_rows * top_k, dtype=jnp.int32) // top_k
    outgoing = jnp.zeros((experts * capacity, half), jnp.bfloat16).at[slot].set(normed[source])
    hidden_width = w_down.shape[1]
    shaped = outgoing.reshape(experts, capacity, half)
    arrived = lax.all_to_all(shaped, ("ep", "tp"), split_axis=0, concat_axis=0, tiled=True)
    width = arrived.shape[1]
    grouped = arrived.reshape(-1, local_experts, width, half)
    both = jnp.einsum("slcd,ldf->slcf", grouped, w_gate_up, preferred_element_type=jnp.float32)
    both = lax.psum(both.astype(jnp.bfloat16), "pool").astype(jnp.float32)
    hidden = (jax.nn.silu(both[..., :hidden_width]) * both[..., hidden_width:]).astype(jnp.bfloat16)
    result = jnp.einsum(
        "slcf,lfd->slcd", hidden, w_down, preferred_element_type=jnp.float32
    ).astype(jnp.bfloat16)
    finished = result.reshape(-1, width, half)
    back = lax.all_to_all(finished, ("ep", "tp"), split_axis=0, concat_axis=0, tiled=True)
    back_rows = back.reshape(experts * capacity, half)[slot]
    gathered = back_rows.reshape(moe_rows, top_k, half).astype(jnp.float32)
    blended = jnp.sum(gathered * mix_weights[:, :, None], axis=1)
    return (hidden_state + blended).astype(jnp.bfloat16)


def solution(mesh):
    placed = (
        P(("grp", "ep"), ("pool", "tp")),
        P(("grp", "ep"), "pool"),
        P(("grp", "ep", "tp"), "pool"),
        P("pool"),
        P(("pool", "tp"), None),
        P(("ep", "tp"), "pool", None),
        P(("ep", "tp"), None, "pool"),
        P(("grp", "ep", "tp"), None),
        P(("grp", "ep", "tp"), None),
        P("grp"),
    )
    return jax.shard_map(
        body, mesh=mesh, in_specs=placed, out_specs=P(("grp", "ep", "tp"), "pool"), check_vma=False
    )
```

```python
import functools
import math

import jax
import jax.numpy as jnp
from jax import lax
from jax.experimental import pallas as pl
from jax.experimental.pallas import tpu as pltpu
from jax.sharding import PartitionSpec as P

D = 2048
QH = 32
KVH = 4
HD = 128


def clip_index(clip_lengths, places):
    ends = jnp.cumsum(clip_lengths)
    return jnp.sum((places[:, None] >= ends[None, :]).astype(jnp.int32), axis=1)


def layer_kernel(
    n_z,
    n_experts,
    parts,
    clip_hbm,
    queries_hbm,
    kv_hbm,
    residual_hbm,
    gain_hbm,
    ids_hbm,
    mix_hbm,
    wo_hbm,
    wgu_hbm,
    wd_hbm,
    out_ref,
    clip_ref,
    queries_ref,
    residual_ref,
    gain_ref,
    ids_ref,
    mix_ref,
    kv,
    attended,
    tops,
    totals,
    numers,
    proj,
    sib_in,
    x_in,
    hidden_ref,
    wo,
    kz_send,
    kz_recv,
    ky_send,
    ky_recv,
    at_send,
    at_recv,
    held,
    wgu,
    wd,
    term,
    pair_in,
    relay_x,
    relay_y,
    from_x,
    from_y,
    from_z,
    w_sem,
    z_send,
    z_recv,
    x_send,
    x_recv,
    y_send,
    y_recv,
    da_send,
    da_recv,
    db_send,
    db_recv,
    sib_send,
    sib_recv,
    pair_send,
    pair_recv,
    r_send,
    r_recv,
    rz_send,
    rz_recv,
):
    ep = lax.axis_index("ep")
    tp = lax.axis_index("tp")
    z, y = ep // 2, ep % 2
    x, c = tp // 2, tp % 2
    rows, half = residual_ref.shape
    cut = half // 2
    quarter = half // 4
    width = held.shape[4]
    q_rows = queries_ref.shape[0]
    first, second, rest = pl.ds(0, cut), pl.ds(cut, cut), pl.ds(cut, width - cut)
    x_peer = (ep, (1 - x) * 2 + c)
    y_peer = (z * 2 + 1 - y, tp)
    sib = (ep, x * 2 + 1 - c)
    q_own, q_x = x * 2 + y, (1 - x) * 2 + y
    q_y, q_d = x * 2 + 1 - y, (1 - x) * 2 + 1 - y

    pair_width = kv.shape[2]
    own_keys = kv_hbm.at[:, pl.ds(pl.multiple_of(tp * pair_width, pair_width), pair_width)]
    loads = [
        pltpu.make_async_copy(src, dst, w_sem.at[number])
        for number, (src, dst) in enumerate(
            (
                (own_keys, kv.at[ep]),
                (queries_hbm, queries_ref),
                (ids_hbm, ids_ref),
                (mix_hbm, mix_ref),
                (residual_hbm, residual_ref),
                (gain_hbm, gain_ref),
                (wo_hbm, wo),
                (wgu_hbm.at[0], wgu),
                (wd_hbm.at[0], wd),
                (clip_hbm, clip_ref),
            )
        )
    ]
    for load in loads:
        load.start()

    barrier = pltpu.get_barrier_semaphore()
    for peer in (x_peer, y_peer, sib):
        pl.semaphore_signal(
            barrier,
            inc=1,
            device_id={"ep": peer[0], "tp": peer[1]},
            device_id_type=pl.DeviceIdType.MESH,
        )
    for step in range(1, n_z):
        pl.semaphore_signal(
            barrier,
            inc=1,
            device_id={"ep": ((z + step) % n_z) * 2 + y, "tp": tp},
            device_id_type=pl.DeviceIdType.MESH,
        )

    def remote(src, dst, send, recv, peer):
        return pltpu.make_async_remote_copy(
            src_ref=src,
            dst_ref=dst,
            send_sem=send,
            recv_sem=recv,
            device_id={"ep": peer[0], "tp": peer[1]},
            device_id_type=pl.DeviceIdType.MESH,
        )

    def along_z(block, up):
        there = z + 1 if up else z - 1
        return remote(
            held.at[q_own, c, block],
            held.at[q_own, c, block],
            z_send.at[1 if up else 0, block],
            z_recv.at[block],
            (there * 2 + y, tp),
        )

    def over_x(q, block):
        here = held.at[q, c, block]
        return remote(here, here, x_send.at[block], x_recv.at[block], x_peer)

    def over_y(q, block):
        here = held.at[q, c, block]
        return remote(here, here, y_send.at[block], y_recv.at[block], y_peer)

    def diag_x(q, block):
        here = held.at[q, c, block, :, first]
        return remote(here, here, da_send.at[block], da_recv.at[block], x_peer)

    def diag_y(q, block):
        here = held.at[q, c, block, :, rest]
        return remote(here, here, db_send.at[block], db_recv.at[block], y_peer)

    def share(q, core, slot, block):
        here = held.at[q, core, block]
        return remote(here, here, sib_send.at[slot, block], sib_recv.at[slot, block], sib)

    def shares_arrive(q, slot):
        for block in range(n_z):
            share(q, 1 - c, slot, block).wait_recv()

    def each_at(distance, act):
        if distance == 0:
            act(z, 0)
            return
        pl.when(z - distance >= 0)(lambda: act(z - distance, -1))
        pl.when(z + distance < n_z)(lambda: act(z + distance, 1))

    def keys_z(block, up):
        there = z + 1 if up else z - 1
        here = kv.at[block * 2 + y]
        return remote(
            here, here, kz_send.at[1 if up else 0, block], kz_recv.at[block], (there * 2 + y, tp)
        )

    def keys_y(block, side_y):
        here = kv.at[block * 2 + side_y]
        return remote(here, here, ky_send.at[block], ky_recv.at[block], y_peer)

    def keys_arrive(block, side):
        if side:
            keys_z(block, side < 0).wait_recv()
        if side <= 0:
            pl.when(z + 1 < n_z)(lambda: keys_z(block, True).start())
        if side >= 0:
            pl.when(z >= 1)(lambda: keys_z(block, False).start())
        keys_y(block, y).start()

    head = pair_width // 2
    loads[0].wait()
    pl.semaphore_wait(barrier, 3 + n_z - 1)
    for distance in range(min(2, n_z)):
        each_at(distance, keys_arrive)

    near = z // (n_z // 2)
    n_keys = n_z * q_rows
    place = lax.broadcasted_iota(jnp.int32, (2 * q_rows, 1), 0)
    place = jnp.where(place >= q_rows, place - q_rows, place) + ep * q_rows
    key_place = lax.broadcasted_iota(jnp.int32, (1, n_keys), 1)
    clip = jnp.zeros(place.shape, jnp.int32)
    key_clips = [jnp.zeros(key_place.shape, jnp.int32) for _ in range(2)]
    key_places = [key_place + near * n_keys, key_place + (1 - near) * n_keys]
    end = jnp.int32(0)
    loads[9].wait()
    for number in range(clip_ref.shape[0]):
        end = end + clip_ref[number]
        clip = clip + jnp.where(place >= end, 1, 0)
        key_clips = [
            key_clip + jnp.where(at >= end, 1, 0) for key_clip, at in zip(key_clips, key_places)
        ]

    loads[2].wait()
    loads[3].wait()
    lane = lax.broadcasted_iota(jnp.int32, (width - half, rows), 0)
    base = jnp.zeros(lane.shape, jnp.int32)
    for part in range(1, parts):
        base = base + jnp.where(lane >= part * n_experts, n_experts, 0)
    wanted = lane - base
    weight = jnp.zeros(lane.shape, jnp.float32)
    for slot in range(ids_ref.shape[0]):
        weight = weight + jnp.where(
            ids_ref[slot : slot + 1, :] == wanted, mix_ref[slot : slot + 1, :], 0.0
        )
    packed = jnp.zeros(lane.shape, jnp.float32)
    for part in range(parts):
        piece = weight.astype(jnp.bfloat16).astype(jnp.float32)
        packed = jnp.where(base == part * n_experts, piece, packed)
        weight = weight - piece
    unit = lax.broadcasted_iota(jnp.int32, (rows, rows), 0) == lax.broadcasted_iota(
        jnp.int32, (rows, rows), 1
    )
    held[q_own, c, z, :, half:width] = lax.dot_general(
        jnp.where(unit, 1.0, 0.0).astype(jnp.bfloat16),
        packed.astype(jnp.bfloat16),
        (((1,), (1,)), ((), ())),
        preferred_element_type=jnp.float32,
    ).astype(jnp.bfloat16)

    loads[1].wait()
    scale = head ** (-0.5) * math.log2(math.e)

    def attend(far):
        side = (1 - near) if far else near
        first_block = pl.ds(side * n_z, n_z)
        keys = kv[first_block, :, 0:head].reshape(n_keys, head)
        values = kv[first_block, :, head:pair_width].reshape(n_keys, head)
        same = clip == key_clips[1 if far else 0]
        for at in range(0, queries_ref.shape[1], 2 * head):
            slot = at // (2 * head)
            two = jnp.concatenate(
                [queries_ref[:, at : at + head], queries_ref[:, at + head : at + 2 * head]],
                axis=0,
            )
            scores = lax.dot_general(
                two, keys, (((1,), (1,)), ((), ())), preferred_element_type=jnp.float32
            )
            scores = jnp.where(same, scores, -1e30)
            top = jnp.max(scores, axis=1, keepdims=True)
            if far:
                top = jnp.maximum(top, tops[slot])
            weights = jnp.exp2((scores - top) * scale)
            total = jnp.sum(weights, axis=1, keepdims=True)
            numer = jnp.dot(
                weights.astype(jnp.bfloat16), values, preferred_element_type=jnp.float32
            )
            if not far:
                tops[slot] = top
                totals[slot] = total
                numers[slot] = numer
                if slot % 2 == 1 and later:
                    each_at(later.pop(0), keys_arrive)
                continue
            factor = jnp.exp2((tops[slot] - top) * scale)
            total = total + totals[slot] * factor
            result = ((numer + numers[slot] * factor) / total).astype(jnp.bfloat16)
            attended[:, at : at + head] = result[0:q_rows]
            attended[:, at + head : at + 2 * head] = result[q_rows : 2 * q_rows]

    half_z = n_z // 2
    for distance in range(2, half_z):
        each_at(distance, keys_arrive)
    for block in range(half_z):
        keys_y(near * half_z + block, 1 - y).wait_recv()
    later = list(range(max(2, half_z), n_z))
    attend(False)
    for distance in later:
        each_at(distance, keys_arrive)
    for block in range(half_z):
        keys_y((1 - near) * half_z + block, 1 - y).wait_recv()
    attend(True)

    def proj_pair(part):
        columns = pl.ds(part * cut, cut)
        return remote(
            proj.at[1 - c, :, :, columns],
            sib_in.at[:, :, columns],
            at_send.at[part],
            at_recv.at[part],
            sib,
        )

    def proj_x(part):
        columns = pl.ds(part * cut, cut)
        return remote(
            proj.at[c, 1 - x, :, columns],
            x_in.at[:, columns],
            at_send.at[2 + part],
            at_recv.at[2 + part],
            x_peer,
        )

    loads[6].wait()
    for part in range(2):
        for at in range(part * cut, (part + 1) * cut, quarter):
            result = jnp.dot(
                attended[...], wo[:, at : at + quarter], preferred_element_type=jnp.float32
            ).astype(jnp.bfloat16)
            for side_x in range(2):
                for side_c in range(2):
                    start = (side_x * 2 + side_c) * rows
                    proj[side_c, side_x, :, at : at + quarter] = result[start : start + rows]
        proj_pair(part).start()
    for part in range(2):
        columns = pl.ds(part * cut, cut)
        proj_pair(part).wait_recv()
        proj[c, 1 - x, :, columns] = (
            proj[c, 1 - x, :, columns].astype(jnp.float32)
            + sib_in[1 - x, :, columns].astype(jnp.float32)
        ).astype(jnp.bfloat16)
        proj_x(part).start()
    loads[4].wait()
    loads[5].wait()
    for part in range(2):
        columns = pl.ds(part * cut, cut)
        hidden_ref[:, columns] = (
            residual_ref[:, columns].astype(jnp.float32)
            + proj[c, x, :, columns].astype(jnp.float32)
            + sib_in[x, :, columns].astype(jnp.float32)
        )
    for part in range(2):
        columns = pl.ds(part * cut, cut)
        proj_x(part).wait_recv()
        hidden_ref[:, columns] += x_in[:, columns].astype(jnp.float32)
    hidden = hidden_ref[...]
    squares = jnp.sum(hidden * hidden, axis=1, keepdims=True) / half
    held[q_own, c, z, :, 0:half] = (hidden * lax.rsqrt(squares + 1e-06) * gain_ref[...]).astype(
        jnp.bfloat16
    )

    def arrive_z(block, side):
        if side:
            along_z(block, side < 0).wait_recv()
        if side <= 0:
            pl.when(z + 1 < n_z)(lambda: along_z(block, True).start())
        if side >= 0:
            pl.when(z >= 1)(lambda: along_z(block, False).start())
        over_x(q_own, block).start()
        over_y(q_own, block).start()
        share(q_own, c, 0, block).start()

    def arrive_xy(block, side):
        over_x(q_x, block).wait_recv()
        diag_y(q_x, block).start()
        share(q_x, c, 1, block).start()
        over_y(q_y, block).wait_recv()
        diag_x(q_y, block).start()
        share(q_y, c, 2, block).start()

    def arrive_diag(block, side):
        diag_x(q_d, block).wait_recv()
        diag_y(q_d, block).wait_recv()
        share(q_d, c, 3, block).start()

    mine = ep * lax.axis_size("tp") + tp
    many = 2 * n_z * rows

    def pair(q, slot, part):
        columns = pl.ds(part * cut, cut)
        return remote(
            term.at[q, 1 - c, :, columns],
            pair_in.at[slot, :, columns],
            pair_send.at[slot, part],
            pair_recv.at[slot, part],
            sib,
        )

    def compute(q, slot):
        both = jnp.dot(
            held[q, :, :, :, 0:half].reshape(many, half),
            wgu[...],
            preferred_element_type=jnp.float32,
        )
        ff = both.shape[1] // 2
        gate, up = both[:, :ff], both[:, ff:]
        acted = (gate / (1.0 + jnp.exp(-gate)) * up).astype(jnp.bfloat16)
        shares = held[q, :, :, :, half:width].reshape(many, width - half).astype(jnp.float32)
        lane = lax.broadcasted_iota(jnp.int32, shares.shape, 1)
        wanted = lane == mine
        for part in range(1, parts):
            wanted = wanted | (lane == mine + part * n_experts)
        mix = jnp.sum(jnp.where(wanted, shares, 0.0), axis=1, keepdims=True)
        tile = half // 4
        for at in range(0, half, tile):
            result = jnp.dot(
                acted, wd[:, at : at + tile], preferred_element_type=jnp.float32
            ).astype(jnp.bfloat16)
            term[q, :, :, at : at + tile] = (
                (result.astype(jnp.float32) * mix)
                .astype(jnp.bfloat16)
                .reshape(2, n_z * rows, tile)
            )
            if (at + tile) % cut == 0:
                pair(q, slot, at // cut).start()

    def add_pair(q, slot, part):
        pair(q, slot, part).wait_recv()
        to = pl.ds(part * cut, cut)
        term[q, c, :, to] = (
            term[q, c, :, to].astype(jnp.float32) + pair_in[slot, :, to].astype(jnp.float32)
        ).astype(jnp.bfloat16)

    def reduce_x(q, columns, into, slot):
        return remote(term.at[q, c, :, columns], into, r_send.at[slot], r_recv.at[slot], x_peer)

    def reduce_y(q, columns, into, slot):
        return remote(term.at[q, c, :, columns], into, r_send.at[slot], r_recv.at[slot], y_peer)

    chunks = from_z.shape[1]
    piece_width = cut // chunks
    low = [pl.ds(i * piece_width, piece_width) for i in range(chunks)]
    high = [pl.ds(cut + i * piece_width, piece_width) for i in range(chunks)]
    own_x = reduce_x(q_x, first, from_x.at[0], 0)
    own_y = reduce_y(q_y, second, from_y.at[1], 1)
    pass_x = [reduce_x(q_d, low[i], relay_x.at[:, low[i]], 2 + i) for i in range(chunks)]
    pass_y = [reduce_y(q_d, high[i], relay_y.at[:, low[i]], 6 + i) for i in range(chunks)]
    last_x = [reduce_x(q_x, high[i], from_x.at[1, :, low[i]], 10 + i) for i in range(chunks)]
    last_y = [reduce_y(q_y, low[i], from_y.at[0, :, low[i]], 14 + i) for i in range(chunks)]

    for distance in range(n_z):
        each_at(distance, arrive_z)
        if distance >= 1:
            each_at(distance - 1, arrive_xy)
    loads[7].wait()
    loads[8].wait()
    shares_arrive(q_own, 0)
    compute(q_own, 0)
    each_at(n_z - 1, arrive_xy)
    shares_arrive(q_x, 1)
    compute(q_x, 1)
    for distance in range(n_z - 2):
        each_at(distance, arrive_diag)
    shares_arrive(q_y, 2)
    add_pair(q_x, 1, 0)
    own_x.start()
    compute(q_y, 2)
    for distance in range(max(n_z - 2, 0), n_z):
        each_at(distance, arrive_diag)
    add_pair(q_y, 2, 1)
    own_y.start()
    shares_arrive(q_d, 3)
    compute(q_d, 3)
    add_pair(q_d, 3, 0)
    for copy in pass_x[:2]:
        copy.start()
    add_pair(q_d, 3, 1)
    for copy in pass_y[:2]:
        copy.start()
    add_pair(q_y, 2, 0)
    add_pair(q_x, 1, 1)
    add_pair(q_own, 0, 0)
    add_pair(q_own, 0, 1)

    def relay(i):
        pass_x[i].wait_recv()
        term[q_y, c, :, low[i]] = (
            term[q_y, c, :, low[i]].astype(jnp.float32) + relay_x[:, low[i]].astype(jnp.float32)
        ).astype(jnp.bfloat16)
        last_y[i].start()
        pass_y[i].wait_recv()
        term[q_x, c, :, high[i]] = (
            term[q_x, c, :, high[i]].astype(jnp.float32) + relay_y[:, low[i]].astype(jnp.float32)
        ).astype(jnp.bfloat16)
        last_x[i].start()
        if i + 2 < chunks:
            pass_x[i + 2].start()
            pass_y[i + 2].start()

    def finish(side, i):
        columns = high[i] if side else low[i]
        term[q_own, c, :, columns] = (
            term[q_own, c, :, columns].astype(jnp.float32)
            + from_x[side, :, low[i]].astype(jnp.float32)
            + from_y[side, :, low[i]].astype(jnp.float32)
        ).astype(jnp.bfloat16)

    def deliver(side, i, step):
        there = (z + step) % n_z
        return remote(
            term.at[
                q_own,
                c,
                pl.ds(pl.multiple_of(there * rows, rows), rows),
                high[i] if side else low[i],
            ],
            from_z.at[side, i, n_z - 1 - step],
            rz_send.at[side, i, step - 1],
            rz_recv.at[side, i, n_z - 1 - step],
            (there * 2 + y, tp),
        )

    def collect(side, i):
        columns = high[i] if side else low[i]
        total = hidden_ref[:, columns] + term[
            q_own, c, pl.ds(pl.multiple_of(z * rows, rows), rows), columns
        ].astype(jnp.float32)
        for step in range(1, n_z):
            deliver(side, i, step).wait_recv()
            total = total + from_z[side, i, n_z - 1 - step].astype(jnp.float32)
        out_ref[:, columns] = total.astype(jnp.bfloat16)

    def complete(i):
        for side in range(2):
            (last_x if side else last_y)[i].wait_recv()
            finish(side, i)
            for step in range(1, n_z):
                deliver(side, i, step).start()

    relay(0)
    own_x.wait_recv()
    own_y.wait_recv()
    for i in range(1, chunks):
        relay(i)
        complete(i - 1)
    complete(chunks - 1)
    for i in range(chunks):
        for side in range(2):
            collect(side, i)

    for copy in [own_x, own_y] + pass_x + pass_y + last_x + last_y:
        copy.wait_send()
    for part in range(2):
        proj_pair(part).wait_send()
        proj_x(part).wait_send()
    for slot, q in enumerate((q_own, q_x, q_y, q_d)):
        for block in range(n_z):
            share(q, c, slot, block).wait_send()
        for part in range(2):
            pair(q, slot, part).wait_send()
    for step in range(1, n_z):
        for i in range(chunks):
            for side in range(2):
                deliver(side, i, step).wait_send()
    for block in range(n_z):
        keys_y(block, y).wait_send()
        pl.when((z + 1 < n_z) & (block <= z))(lambda: keys_z(block, True).wait_send())
        pl.when((z >= 1) & (block >= z))(lambda: keys_z(block, False).wait_send())
        over_x(q_own, block).wait_send()
        over_y(q_own, block).wait_send()
        diag_x(q_y, block).wait_send()
        diag_y(q_x, block).wait_send()
        pl.when((z + 1 < n_z) & (block <= z))(lambda: along_z(block, True).wait_send())
        pl.when((z >= 1) & (block >= z))(lambda: along_z(block, False).wait_send())


def whole_layer(
    queries,
    keys_values,
    residual,
    norm_gain,
    w_out,
    w_gate_up,
    w_down,
    expert_ids,
    mix_weights,
    clip_lengths,
):
    n_ep = lax.axis_size("ep")
    n_z = n_ep // 2
    n_experts = n_ep * lax.axis_size("tp")
    rows, half = residual.shape
    q_rows = queries.shape[0]
    parts = 3
    width = half + -(-parts * n_experts // 128) * 128
    many = n_z * rows
    cut = half // 2
    chunks = 4
    dma = pltpu.SemaphoreType.DMA
    bf16 = jnp.bfloat16
    in_vmem = pl.BlockSpec(memory_space=pltpu.VMEM)
    return pl.pallas_call(
        functools.partial(layer_kernel, n_z, n_experts, parts),
        out_shape=jax.ShapeDtypeStruct((rows, half), bf16),
        in_specs=[pl.BlockSpec(memory_space=pltpu.HBM)] * 10,
        out_specs=in_vmem,
        scratch_shapes=[
            pltpu.SMEM(clip_lengths.shape, jnp.int32),
            pltpu.VMEM(queries.shape, bf16),
            pltpu.VMEM(residual.shape, bf16),
            pltpu.VMEM((1, half), jnp.float32),
            pltpu.VMEM(expert_ids.shape[::-1], jnp.int32),
            pltpu.VMEM(mix_weights.shape[::-1], jnp.float32),
            pltpu.VMEM((n_ep, q_rows, 2 * HD), bf16),
            pltpu.VMEM(queries.shape, bf16),
            pltpu.VMEM((queries.shape[1] // (2 * HD), 2 * q_rows, 1), jnp.float32),
            pltpu.VMEM((queries.shape[1] // (2 * HD), 2 * q_rows, 1), jnp.float32),
            pltpu.VMEM((queries.shape[1] // (2 * HD), 2 * q_rows, HD), jnp.float32),
            pltpu.VMEM((2, 2, rows, half), bf16),
            pltpu.VMEM((2, rows, half), bf16),
            pltpu.VMEM((rows, half), bf16),
            pltpu.VMEM((rows, half), jnp.float32),
            pltpu.VMEM(w_out.shape, bf16),
            dma((2, n_z)),
            dma((n_z,)),
            dma((n_z,)),
            dma((n_z,)),
            dma((4,)),
            dma((4,)),
            pltpu.VMEM((4, 2, n_z, rows, width), bf16),
            pltpu.VMEM(w_gate_up.shape[1:], bf16),
            pltpu.VMEM(w_down.shape[1:], bf16),
            pltpu.VMEM((4, 2, many, half), bf16),
            pltpu.VMEM((4, many, half), bf16),
            pltpu.VMEM((many, cut), bf16),
            pltpu.VMEM((many, cut), bf16),
            pltpu.VMEM((2, many, cut), bf16),
            pltpu.VMEM((2, many, cut), bf16),
            pltpu.VMEM((2, chunks, n_z - 1, rows, cut // chunks), bf16),
            dma((10,)),
            dma((2, n_z)),
        ]
        + [dma((n_z,))] * 9
        + [dma((4, n_z))] * 2
        + [dma((4, 2))] * 2
        + [dma((2 + 4 * chunks,))] * 2
        + [dma((2, chunks, n_z - 1))] * 2,
        compiler_params=pltpu.CompilerParams(
            collective_id=0, has_side_effects=True, vmem_limit_bytes=62 * 1024 * 1024
        ),
    )(
        clip_lengths,
        queries,
        keys_values,
        residual,
        norm_gain.reshape(1, half),
        expert_ids.T,
        mix_weights.T,
        w_out,
        w_gate_up,
        w_down,
    )


def body(
    queries,
    keys_values,
    residual,
    norm_gain,
    w_out,
    w_gate_up,
    w_down,
    expert_ids,
    mix_weights,
    clip_lengths,
):
    rows = queries.shape[0]
    heads_here = queries.shape[1] // HD
    if (
        lax.axis_size("pool") == 1
        and lax.axis_size("tp") == 4
        and lax.axis_size("ep") % 4 == 0
        and heads_here == QH // KVH
        and w_gate_up.shape[0] == 1
        and residual.shape[0] % 16 == 0
        and residual.shape[1] == D
        and rows == 4 * residual.shape[0]
    ):
        return whole_layer(
            queries,
            keys_values,
            residual,
            norm_gain,
            w_out,
            w_gate_up,
            w_down,
            expert_ids,
            mix_weights,
            clip_lengths,
        )
    pool_size = lax.axis_size("pool")
    tensor_size = lax.axis_size("tp")
    context_size = lax.axis_size("ep")
    pool_index = lax.axis_index("pool")
    tensor_index = lax.axis_index("tp")
    pair_heads = keys_values.shape[1] // (2 * HD)
    group = QH // KVH
    head_pick = (
        pool_index * tensor_size + tensor_index
    ) * heads_here // group - pool_index * pair_heads
    own_pairs = lax.dynamic_slice_in_dim(keys_values, head_pick * (2 * HD), 2 * HD, 1)
    places = lax.axis_index("ep") * rows + jnp.arange(rows, dtype=jnp.int32)
    query_clip = clip_index(clip_lengths, places)
    query_heads = queries.reshape(rows, heads_here, HD)
    scale = HD ** (-0.5)
    start_state = (
        jnp.full((heads_here, rows), -1e30, jnp.float32),
        jnp.zeros((heads_here, rows), jnp.float32),
        jnp.zeros((heads_here, rows, HD), jnp.float32),
    )
    piece = lax.all_gather(own_pairs, "ep", axis=0, tiled=True)
    length = piece.shape[0]
    stride = min(length, rows * max(1, 512 // rows))
    while length % stride:
        stride = stride - 1

    def one_block(index, state):
        top, total, numer = state
        block = lax.dynamic_slice_in_dim(piece, index * stride, stride, 0)
        key_clip = clip_index(clip_lengths, index * stride + jnp.arange(stride, dtype=jnp.int32))
        scores = (
            jnp.einsum(
                "rhd,nd->hrn", query_heads, block[:, :HD], preferred_element_type=jnp.float32
            )
            * scale
        )
        same = (query_clip[:, None] == key_clip[None, :])[None, :, :]
        new_top = jnp.maximum(top, jnp.max(jnp.where(same, scores, -1e30), axis=2))
        weights = jnp.where(same, jnp.exp(scores - new_top[:, :, None]), 0.0)
        factor = jnp.exp(top - new_top)
        total = total * factor + jnp.sum(weights, axis=2)
        numer = numer * factor[:, :, None] + jnp.einsum(
            "hrn,nd->hrd",
            weights.astype(jnp.bfloat16),
            block[:, HD:],
            preferred_element_type=jnp.float32,
        )
        return (new_top, total, numer)

    top, total, numer = lax.fori_loop(0, length // stride, one_block, start_state)
    attended = (numer / total[:, :, None]).astype(jnp.bfloat16)
    half = residual.shape[1]
    out_heads = w_out.reshape(heads_here, HD, pool_size * half)
    moe_rows = residual.shape[0]
    start = jnp.int32(0)
    pieces = []
    for offset in range(lax.axis_size(("pool", "tp")) * moe_rows // rows):
        part = start // rows + offset
        weights = lax.dynamic_slice_in_dim(out_heads, part * half, half, 2)
        pieces.append(
            jnp.einsum("hrd,hde->re", attended, weights, preferred_element_type=jnp.float32)
        )
    mixed = lax.psum_scatter(
        jnp.concatenate(pieces, axis=0).astype(jnp.bfloat16),
        ("pool", "tp"),
        scatter_dimension=0,
        tiled=True,
    ).astype(jnp.float32)
    hidden_state = residual.astype(jnp.float32) + mixed
    squares = lax.psum(jnp.sum(hidden_state * hidden_state, axis=1), "pool")
    normed = (hidden_state * lax.rsqrt(squares / D + 1e-06)[:, None] * norm_gain[None, :]).astype(
        jnp.bfloat16
    )
    top_k = expert_ids.shape[1]
    local_experts = w_gate_up.shape[0]
    experts = local_experts * context_size * tensor_size
    capacity = 2 * moe_rows * top_k // experts
    flat = expert_ids.reshape(-1)
    marks = (flat[:, None] == jnp.arange(experts, dtype=jnp.int32)[None, :]).astype(jnp.int32)
    rank = jnp.sum(jnp.cumsum(marks, axis=0) * marks, axis=1) - 1
    slot = flat * capacity + rank
    source = jnp.arange(moe_rows * top_k, dtype=jnp.int32) // top_k
    outgoing = jnp.zeros((experts * capacity, half), jnp.bfloat16).at[slot].set(normed[source])
    hidden_width = w_down.shape[1]
    shaped = outgoing.reshape(experts, capacity, half)
    arrived = lax.all_to_all(shaped, ("ep", "tp"), split_axis=0, concat_axis=0, tiled=True)
    width = arrived.shape[1]
    grouped = arrived.reshape(-1, local_experts, width, half)
    both = jnp.einsum("slcd,ldf->slcf", grouped, w_gate_up, preferred_element_type=jnp.float32)
    both = lax.psum(both.astype(jnp.bfloat16), "pool").astype(jnp.float32)
    hidden = (jax.nn.silu(both[..., :hidden_width]) * both[..., hidden_width:]).astype(jnp.bfloat16)
    result = jnp.einsum(
        "slcf,lfd->slcd", hidden, w_down, preferred_element_type=jnp.float32
    ).astype(jnp.bfloat16)
    finished = result.reshape(-1, width, half)
    back = lax.all_to_all(finished, ("ep", "tp"), split_axis=0, concat_axis=0, tiled=True)
    back_rows = back.reshape(experts * capacity, half)[slot]
    gathered = back_rows.reshape(moe_rows, top_k, half).astype(jnp.float32)
    blended = jnp.sum(gathered * mix_weights[:, :, None], axis=1)
    return (hidden_state + blended).astype(jnp.bfloat16)


def solution(mesh):
    placed = (
        P(("grp", "ep"), ("pool", "tp")),
        P(("grp", "ep"), "pool"),
        P(("grp", "ep", "tp"), "pool"),
        P("pool"),
        P(("pool", "tp"), None),
        P(("ep", "tp"), "pool", None),
        P(("ep", "tp"), None, "pool"),
        P(("grp", "ep", "tp"), None),
        P(("grp", "ep", "tp"), None),
        P("grp"),
    )
    return jax.shard_map(
        body, mesh=mesh, in_specs=placed, out_specs=P(("grp", "ep", "tp"), "pool"), check_vma=False
    )
```

```python
import functools
import math

import jax
import jax.numpy as jnp
from jax import lax
from jax.experimental import pallas as pl
from jax.experimental.pallas import tpu as pltpu
from jax.sharding import PartitionSpec as P

D = 2048
QH = 32
KVH = 4
HD = 128


def clip_index(clip_lengths, places):
    ends = jnp.cumsum(clip_lengths)
    return jnp.sum((places[:, None] >= ends[None, :]).astype(jnp.int32), axis=1)


def layer_kernel(
    n_z,
    n_experts,
    parts,
    clip_hbm,
    queries_hbm,
    kv_hbm,
    residual_hbm,
    gain_hbm,
    ids_hbm,
    mix_hbm,
    wo_hbm,
    wgu_hbm,
    wd_hbm,
    out_ref,
    clip_ref,
    queries_ref,
    residual_ref,
    gain_ref,
    ids_ref,
    mix_ref,
    kv,
    attended,
    proj,
    sib_in,
    x_in,
    hidden_ref,
    wo,
    kz_send,
    kz_recv,
    ky_send,
    ky_recv,
    at_send,
    at_recv,
    held,
    wgu,
    wd,
    term,
    pair_in,
    relay_x,
    relay_y,
    from_x,
    from_y,
    from_z,
    w_sem,
    z_send,
    z_recv,
    x_send,
    x_recv,
    y_send,
    y_recv,
    da_send,
    da_recv,
    db_send,
    db_recv,
    sib_send,
    sib_recv,
    pair_send,
    pair_recv,
    r_send,
    r_recv,
    rz_send,
    rz_recv,
):
    ep = lax.axis_index("ep")
    tp = lax.axis_index("tp")
    z, y = ep // 2, ep % 2
    x, c = tp // 2, tp % 2
    rows, half = residual_ref.shape
    cut = half // 2
    quarter = half // 4
    width = held.shape[4]
    q_rows = queries_ref.shape[0]
    first, second, rest = pl.ds(0, cut), pl.ds(cut, cut), pl.ds(cut, width - cut)
    x_peer = (ep, (1 - x) * 2 + c)
    y_peer = (z * 2 + 1 - y, tp)
    sib = (ep, x * 2 + 1 - c)
    q_own, q_x = x * 2 + y, (1 - x) * 2 + y
    q_y, q_d = x * 2 + 1 - y, (1 - x) * 2 + 1 - y

    pair_width = kv.shape[2]
    own_keys = kv_hbm.at[:, pl.ds(pl.multiple_of(tp * pair_width, pair_width), pair_width)]
    loads = [
        pltpu.make_async_copy(src, dst, w_sem.at[number])
        for number, (src, dst) in enumerate(
            (
                (own_keys, kv.at[ep]),
                (queries_hbm, queries_ref),
                (ids_hbm, ids_ref),
                (mix_hbm, mix_ref),
                (residual_hbm, residual_ref),
                (gain_hbm, gain_ref),
                (wo_hbm, wo),
                (wgu_hbm.at[0], wgu),
                (wd_hbm.at[0], wd),
                (clip_hbm, clip_ref),
            )
        )
    ]
    for load in loads:
        load.start()

    barrier = pltpu.get_barrier_semaphore()
    for peer in (x_peer, y_peer, sib):
        pl.semaphore_signal(
            barrier,
            inc=1,
            device_id={"ep": peer[0], "tp": peer[1]},
            device_id_type=pl.DeviceIdType.MESH,
        )
    for step in range(1, n_z):
        pl.semaphore_signal(
            barrier,
            inc=1,
            device_id={"ep": ((z + step) % n_z) * 2 + y, "tp": tp},
            device_id_type=pl.DeviceIdType.MESH,
        )

    def remote(src, dst, send, recv, peer):
        return pltpu.make_async_remote_copy(
            src_ref=src,
            dst_ref=dst,
            send_sem=send,
            recv_sem=recv,
            device_id={"ep": peer[0], "tp": peer[1]},
            device_id_type=pl.DeviceIdType.MESH,
        )

    def along_z(block, up):
        there = z + 1 if up else z - 1
        return remote(
            held.at[q_own, c, block],
            held.at[q_own, c, block],
            z_send.at[1 if up else 0, block],
            z_recv.at[block],
            (there * 2 + y, tp),
        )

    def over_x(q, block):
        here = held.at[q, c, block]
        return remote(here, here, x_send.at[block], x_recv.at[block], x_peer)

    def over_y(q, block):
        here = held.at[q, c, block]
        return remote(here, here, y_send.at[block], y_recv.at[block], y_peer)

    def diag_x(q, block):
        here = held.at[q, c, block, :, first]
        return remote(here, here, da_send.at[block], da_recv.at[block], x_peer)

    def diag_y(q, block):
        here = held.at[q, c, block, :, rest]
        return remote(here, here, db_send.at[block], db_recv.at[block], y_peer)

    def share(q, core, slot, block):
        here = held.at[q, core, block]
        return remote(here, here, sib_send.at[slot, block], sib_recv.at[slot, block], sib)

    def shares_arrive(q, slot):
        for block in range(n_z):
            share(q, 1 - c, slot, block).wait_recv()

    def each_at(distance, act):
        if distance == 0:
            act(z, 0)
            return
        pl.when(z - distance >= 0)(lambda: act(z - distance, -1))
        pl.when(z + distance < n_z)(lambda: act(z + distance, 1))

    def keys_z(step):
        there = (z + step) % n_z
        return remote(
            kv.at[ep], kv.at[ep], kz_send.at[step], kz_recv.at[z], (there * 2 + y, tp)
        )

    def keys_from(block):
        here = kv.at[block * 2 + y]
        return remote(here, here, kz_send.at[0], kz_recv.at[block], y_peer)

    def keys_y(block, side_y):
        here = kv.at[block * 2 + side_y]
        return remote(here, here, ky_send.at[block], ky_recv.at[block], y_peer)

    def keys_arrive(block, side):
        if side:
            keys_from(block).wait_recv()
        keys_y(block, y).start()

    head = pair_width // 2
    loads[0].wait()
    pl.semaphore_wait(barrier, 3 + n_z - 1)
    for step in sorted(range(1, n_z), key=lambda step: min(step, n_z - step)):
        keys_z(step).start()
    for distance in range(n_z):
        each_at(distance, keys_arrive)

    n_keys = 2 * n_z * q_rows
    place = lax.broadcasted_iota(jnp.int32, (2 * q_rows, 1), 0)
    place = jnp.where(place >= q_rows, place - q_rows, place) + ep * q_rows
    key_place = lax.broadcasted_iota(jnp.int32, (1, n_keys), 1)
    clip = jnp.zeros(place.shape, jnp.int32)
    key_clip = jnp.zeros(key_place.shape, jnp.int32)
    end = jnp.int32(0)
    loads[9].wait()
    for number in range(clip_ref.shape[0]):
        end = end + clip_ref[number]
        clip = clip + jnp.where(place >= end, 1, 0)
        key_clip = key_clip + jnp.where(key_place >= end, 1, 0)
    same = clip == key_clip

    loads[2].wait()
    loads[3].wait()
    lane = lax.broadcasted_iota(jnp.int32, (width - half, rows), 0)
    base = jnp.zeros(lane.shape, jnp.int32)
    for part in range(1, parts):
        base = base + jnp.where(lane >= part * n_experts, n_experts, 0)
    wanted = lane - base
    weight = jnp.zeros(lane.shape, jnp.float32)
    for slot in range(ids_ref.shape[0]):
        weight = weight + jnp.where(
            ids_ref[slot : slot + 1, :] == wanted, mix_ref[slot : slot + 1, :], 0.0
        )
    packed = jnp.zeros(lane.shape, jnp.float32)
    for part in range(parts):
        piece = weight.astype(jnp.bfloat16).astype(jnp.float32)
        packed = jnp.where(base == part * n_experts, piece, packed)
        weight = weight - piece
    unit = lax.broadcasted_iota(jnp.int32, (rows, rows), 0) == lax.broadcasted_iota(
        jnp.int32, (rows, rows), 1
    )
    held[q_own, c, z, :, half:width] = lax.dot_general(
        jnp.where(unit, 1.0, 0.0).astype(jnp.bfloat16),
        packed.astype(jnp.bfloat16),
        (((1,), (1,)), ((), ())),
        preferred_element_type=jnp.float32,
    ).astype(jnp.bfloat16)

    loads[1].wait()
    for block in range(n_z):
        keys_y(block, 1 - y).wait_recv()
    keys = kv[:, :, 0:head].reshape(n_keys, head)
    values = kv[:, :, head:pair_width].reshape(n_keys, head)
    scale = head ** (-0.5) * math.log2(math.e)
    for at in range(0, queries_ref.shape[1], 2 * head):
        two = jnp.concatenate(
            [queries_ref[:, at : at + head], queries_ref[:, at + head : at + 2 * head]], axis=0
        )
        scores = lax.dot_general(
            two, keys, (((1,), (1,)), ((), ())), preferred_element_type=jnp.float32
        )
        scores = jnp.where(same, scores, -1e30)
        top = jnp.max(scores, axis=1, keepdims=True)
        weights = jnp.exp2((scores - top) * scale)
        total = jnp.sum(weights, axis=1, keepdims=True)
        numer = jnp.dot(
            weights.astype(jnp.bfloat16), values, preferred_element_type=jnp.float32
        )
        result = (numer / total).astype(jnp.bfloat16)
        attended[:, at : at + head] = result[0:q_rows]
        attended[:, at + head : at + 2 * head] = result[q_rows : 2 * q_rows]

    def proj_pair(part):
        columns = pl.ds(part * quarter, quarter)
        return remote(
            proj.at[1 - c, :, :, columns],
            sib_in.at[:, :, columns],
            at_send.at[part],
            at_recv.at[part],
            sib,
        )

    def proj_x(part):
        columns = pl.ds(part * quarter, quarter)
        return remote(
            proj.at[c, 1 - x, :, columns],
            x_in.at[:, columns],
            at_send.at[4 + part],
            at_recv.at[4 + part],
            x_peer,
        )

    loads[6].wait()
    for part in range(4):
        for at in [part * quarter]:
            result = jnp.dot(
                attended[...], wo[:, at : at + quarter], preferred_element_type=jnp.float32
            ).astype(jnp.bfloat16)
            for side_x in range(2):
                for side_c in range(2):
                    start = (side_x * 2 + side_c) * rows
                    proj[side_c, side_x, :, at : at + quarter] = result[start : start + rows]
        proj_pair(part).start()
    for part in range(4):
        columns = pl.ds(part * quarter, quarter)
        proj_pair(part).wait_recv()
        proj[c, 1 - x, :, columns] = (
            proj[c, 1 - x, :, columns].astype(jnp.float32)
            + sib_in[1 - x, :, columns].astype(jnp.float32)
        ).astype(jnp.bfloat16)
        proj_x(part).start()
    loads[4].wait()
    loads[5].wait()
    for part in range(4):
        columns = pl.ds(part * quarter, quarter)
        hidden_ref[:, columns] = (
            residual_ref[:, columns].astype(jnp.float32)
            + proj[c, x, :, columns].astype(jnp.float32)
            + sib_in[x, :, columns].astype(jnp.float32)
        )
    for part in range(4):
        columns = pl.ds(part * quarter, quarter)
        proj_x(part).wait_recv()
        hidden_ref[:, columns] += x_in[:, columns].astype(jnp.float32)
    hidden = hidden_ref[...]
    squares = jnp.sum(hidden * hidden, axis=1, keepdims=True) / half
    held[q_own, c, z, :, 0:half] = (hidden * lax.rsqrt(squares + 1e-06) * gain_ref[...]).astype(
        jnp.bfloat16
    )

    def arrive_z(block, side):
        if side:
            along_z(block, side < 0).wait_recv()
        if side <= 0:
            pl.when(z + 1 < n_z)(lambda: along_z(block, True).start())
        if side >= 0:
            pl.when(z >= 1)(lambda: along_z(block, False).start())
        over_x(q_own, block).start()
        over_y(q_own, block).start()
        share(q_own, c, 0, block).start()

    def arrive_xy(block, side):
        over_x(q_x, block).wait_recv()
        diag_y(q_x, block).start()
        share(q_x, c, 1, block).start()
        over_y(q_y, block).wait_recv()
        diag_x(q_y, block).start()
        share(q_y, c, 2, block).start()

    def arrive_diag(block, side):
        diag_x(q_d, block).wait_recv()
        diag_y(q_d, block).wait_recv()
        share(q_d, c, 3, block).start()

    mine = ep * lax.axis_size("tp") + tp
    many = 2 * n_z * rows

    def pair(q, slot, part):
        columns = pl.ds(part * cut, cut)
        return remote(
            term.at[q, 1 - c, :, columns],
            pair_in.at[slot, :, columns],
            pair_send.at[slot, part],
            pair_recv.at[slot, part],
            sib,
        )

    def compute(q, slot):
        both = jnp.dot(
            held[q, :, :, :, 0:half].reshape(many, half),
            wgu[...],
            preferred_element_type=jnp.float32,
        )
        ff = both.shape[1] // 2
        gate, up = both[:, :ff], both[:, ff:]
        acted = (gate / (1.0 + jnp.exp(-gate)) * up).astype(jnp.bfloat16)
        shares = held[q, :, :, :, half:width].reshape(many, width - half).astype(jnp.float32)
        lane = lax.broadcasted_iota(jnp.int32, shares.shape, 1)
        wanted = lane == mine
        for part in range(1, parts):
            wanted = wanted | (lane == mine + part * n_experts)
        mix = jnp.sum(jnp.where(wanted, shares, 0.0), axis=1, keepdims=True)
        tile = half // 4
        for at in range(0, half, tile):
            result = jnp.dot(
                acted, wd[:, at : at + tile], preferred_element_type=jnp.float32
            ).astype(jnp.bfloat16)
            term[q, :, :, at : at + tile] = (
                (result.astype(jnp.float32) * mix)
                .astype(jnp.bfloat16)
                .reshape(2, n_z * rows, tile)
            )
            if (at + tile) % cut == 0:
                pair(q, slot, at // cut).start()

    def add_pair(q, slot, part):
        pair(q, slot, part).wait_recv()
        to = pl.ds(part * cut, cut)
        term[q, c, :, to] = (
            term[q, c, :, to].astype(jnp.float32) + pair_in[slot, :, to].astype(jnp.float32)
        ).astype(jnp.bfloat16)

    def reduce_x(q, columns, into, slot):
        return remote(term.at[q, c, :, columns], into, r_send.at[slot], r_recv.at[slot], x_peer)

    def reduce_y(q, columns, into, slot):
        return remote(term.at[q, c, :, columns], into, r_send.at[slot], r_recv.at[slot], y_peer)

    chunks = from_z.shape[1]
    piece_width = cut // chunks
    low = [pl.ds(i * piece_width, piece_width) for i in range(chunks)]
    high = [pl.ds(cut + i * piece_width, piece_width) for i in range(chunks)]
    own_x = reduce_x(q_x, first, from_x.at[0], 0)
    own_y = reduce_y(q_y, second, from_y.at[1], 1)
    pass_x = [reduce_x(q_d, low[i], relay_x.at[:, low[i]], 2 + i) for i in range(chunks)]
    pass_y = [reduce_y(q_d, high[i], relay_y.at[:, low[i]], 6 + i) for i in range(chunks)]
    last_x = [reduce_x(q_x, high[i], from_x.at[1, :, low[i]], 10 + i) for i in range(chunks)]
    last_y = [reduce_y(q_y, low[i], from_y.at[0, :, low[i]], 14 + i) for i in range(chunks)]

    for distance in range(n_z):
        each_at(distance, arrive_z)
        if distance >= 1:
            each_at(distance - 1, arrive_xy)
    loads[7].wait()
    loads[8].wait()
    shares_arrive(q_own, 0)
    compute(q_own, 0)
    each_at(n_z - 1, arrive_xy)
    shares_arrive(q_x, 1)
    compute(q_x, 1)
    for distance in range(n_z - 2):
        each_at(distance, arrive_diag)
    shares_arrive(q_y, 2)
    add_pair(q_x, 1, 0)
    own_x.start()
    compute(q_y, 2)
    for distance in range(max(n_z - 2, 0), n_z):
        each_at(distance, arrive_diag)
    add_pair(q_y, 2, 1)
    own_y.start()
    shares_arrive(q_d, 3)
    compute(q_d, 3)
    add_pair(q_d, 3, 0)
    for copy in pass_x[:2]:
        copy.start()
    add_pair(q_d, 3, 1)
    for copy in pass_y[:2]:
        copy.start()
    add_pair(q_y, 2, 0)
    add_pair(q_x, 1, 1)
    add_pair(q_own, 0, 0)
    add_pair(q_own, 0, 1)

    def relay(i):
        pass_x[i].wait_recv()
        term[q_y, c, :, low[i]] = (
            term[q_y, c, :, low[i]].astype(jnp.float32) + relay_x[:, low[i]].astype(jnp.float32)
        ).astype(jnp.bfloat16)
        last_y[i].start()
        pass_y[i].wait_recv()
        term[q_x, c, :, high[i]] = (
            term[q_x, c, :, high[i]].astype(jnp.float32) + relay_y[:, low[i]].astype(jnp.float32)
        ).astype(jnp.bfloat16)
        last_x[i].start()
        if i + 2 < chunks:
            pass_x[i + 2].start()
            pass_y[i + 2].start()

    def finish(side, i):
        columns = high[i] if side else low[i]
        term[q_own, c, :, columns] = (
            term[q_own, c, :, columns].astype(jnp.float32)
            + from_x[side, :, low[i]].astype(jnp.float32)
            + from_y[side, :, low[i]].astype(jnp.float32)
        ).astype(jnp.bfloat16)

    def deliver(side, i, step):
        there = (z + step) % n_z
        return remote(
            term.at[
                q_own,
                c,
                pl.ds(pl.multiple_of(there * rows, rows), rows),
                high[i] if side else low[i],
            ],
            from_z.at[side, i, n_z - 1 - step],
            rz_send.at[side, i, step - 1],
            rz_recv.at[side, i, n_z - 1 - step],
            (there * 2 + y, tp),
        )

    def collect(side, i):
        columns = high[i] if side else low[i]
        total = hidden_ref[:, columns] + term[
            q_own, c, pl.ds(pl.multiple_of(z * rows, rows), rows), columns
        ].astype(jnp.float32)
        for step in range(1, n_z):
            deliver(side, i, step).wait_recv()
            total = total + from_z[side, i, n_z - 1 - step].astype(jnp.float32)
        out_ref[:, columns] = total.astype(jnp.bfloat16)

    def complete(i):
        for side in range(2):
            (last_x if side else last_y)[i].wait_recv()
            finish(side, i)
            for step in range(1, n_z):
                deliver(side, i, step).start()

    relay(0)
    own_x.wait_recv()
    own_y.wait_recv()
    for i in range(1, chunks):
        relay(i)
        complete(i - 1)
    complete(chunks - 1)
    for i in range(chunks):
        for side in range(2):
            collect(side, i)

    for copy in [own_x, own_y] + pass_x + pass_y + last_x + last_y:
        copy.wait_send()
    for step in range(1, n_z):
        keys_z(step).wait_send()
    for part in range(4):
        proj_pair(part).wait_send()
        proj_x(part).wait_send()
    for slot, q in enumerate((q_own, q_x, q_y, q_d)):
        for block in range(n_z):
            share(q, c, slot, block).wait_send()
        for part in range(2):
            pair(q, slot, part).wait_send()
    for step in range(1, n_z):
        for i in range(chunks):
            for side in range(2):
                deliver(side, i, step).wait_send()
    for block in range(n_z):
        keys_y(block, y).wait_send()
        over_x(q_own, block).wait_send()
        over_y(q_own, block).wait_send()
        diag_x(q_y, block).wait_send()
        diag_y(q_x, block).wait_send()
        pl.when((z + 1 < n_z) & (block <= z))(lambda: along_z(block, True).wait_send())
        pl.when((z >= 1) & (block >= z))(lambda: along_z(block, False).wait_send())


def whole_layer(
    queries,
    keys_values,
    residual,
    norm_gain,
    w_out,
    w_gate_up,
    w_down,
    expert_ids,
    mix_weights,
    clip_lengths,
):
    n_ep = lax.axis_size("ep")
    n_z = n_ep // 2
    n_experts = n_ep * lax.axis_size("tp")
    rows, half = residual.shape
    q_rows = queries.shape[0]
    parts = 3
    width = half + -(-parts * n_experts // 128) * 128
    many = n_z * rows
    cut = half // 2
    chunks = 4
    dma = pltpu.SemaphoreType.DMA
    bf16 = jnp.bfloat16
    in_vmem = pl.BlockSpec(memory_space=pltpu.VMEM)
    return pl.pallas_call(
        functools.partial(layer_kernel, n_z, n_experts, parts),
        out_shape=jax.ShapeDtypeStruct((rows, half), bf16),
        in_specs=[pl.BlockSpec(memory_space=pltpu.HBM)] * 10,
        out_specs=in_vmem,
        scratch_shapes=[
            pltpu.SMEM(clip_lengths.shape, jnp.int32),
            pltpu.VMEM(queries.shape, bf16),
            pltpu.VMEM(residual.shape, bf16),
            pltpu.VMEM((1, half), jnp.float32),
            pltpu.VMEM(expert_ids.shape[::-1], jnp.int32),
            pltpu.VMEM(mix_weights.shape[::-1], jnp.float32),
            pltpu.VMEM((n_ep, q_rows, 2 * HD), bf16),
            pltpu.VMEM(queries.shape, bf16),
            pltpu.VMEM((2, 2, rows, half), bf16),
            pltpu.VMEM((2, rows, half), bf16),
            pltpu.VMEM((rows, half), bf16),
            pltpu.VMEM((rows, half), jnp.float32),
            pltpu.VMEM(w_out.shape, bf16),
            dma((n_z,)),
            dma((n_z,)),
            dma((n_z,)),
            dma((n_z,)),
            dma((8,)),
            dma((8,)),
            pltpu.VMEM((4, 2, n_z, rows, width), bf16),
            pltpu.VMEM(w_gate_up.shape[1:], bf16),
            pltpu.VMEM(w_down.shape[1:], bf16),
            pltpu.VMEM((4, 2, many, half), bf16),
            pltpu.VMEM((4, many, half), bf16),
            pltpu.VMEM((many, cut), bf16),
            pltpu.VMEM((many, cut), bf16),
            pltpu.VMEM((2, many, cut), bf16),
            pltpu.VMEM((2, many, cut), bf16),
            pltpu.VMEM((2, chunks, n_z - 1, rows, cut // chunks), bf16),
            dma((10,)),
            dma((2, n_z)),
        ]
        + [dma((n_z,))] * 9
        + [dma((4, n_z))] * 2
        + [dma((4, 2))] * 2
        + [dma((2 + 4 * chunks,))] * 2
        + [dma((2, chunks, n_z - 1))] * 2,
        compiler_params=pltpu.CompilerParams(
            collective_id=0, has_side_effects=True, vmem_limit_bytes=62 * 1024 * 1024
        ),
    )(
        clip_lengths,
        queries,
        keys_values,
        residual,
        norm_gain.reshape(1, half),
        expert_ids.T,
        mix_weights.T,
        w_out,
        w_gate_up,
        w_down,
    )


def body(
    queries,
    keys_values,
    residual,
    norm_gain,
    w_out,
    w_gate_up,
    w_down,
    expert_ids,
    mix_weights,
    clip_lengths,
):
    rows = queries.shape[0]
    heads_here = queries.shape[1] // HD
    if (
        lax.axis_size("pool") == 1
        and lax.axis_size("tp") == 4
        and lax.axis_size("ep") % 2 == 0
        and lax.axis_size("ep") > 2
        and heads_here == QH // KVH
        and w_gate_up.shape[0] == 1
        and residual.shape[0] % 16 == 0
        and residual.shape[1] == D
        and rows == 4 * residual.shape[0]
    ):
        return whole_layer(
            queries,
            keys_values,
            residual,
            norm_gain,
            w_out,
            w_gate_up,
            w_down,
            expert_ids,
            mix_weights,
            clip_lengths,
        )
    pool_size = lax.axis_size("pool")
    tensor_size = lax.axis_size("tp")
    context_size = lax.axis_size("ep")
    pool_index = lax.axis_index("pool")
    tensor_index = lax.axis_index("tp")
    pair_heads = keys_values.shape[1] // (2 * HD)
    group = QH // KVH
    head_pick = (
        pool_index * tensor_size + tensor_index
    ) * heads_here // group - pool_index * pair_heads
    own_pairs = lax.dynamic_slice_in_dim(keys_values, head_pick * (2 * HD), 2 * HD, 1)
    places = lax.axis_index("ep") * rows + jnp.arange(rows, dtype=jnp.int32)
    query_clip = clip_index(clip_lengths, places)
    query_heads = queries.reshape(rows, heads_here, HD)
    scale = HD ** (-0.5)
    start_state = (
        jnp.full((heads_here, rows), -1e30, jnp.float32),
        jnp.zeros((heads_here, rows), jnp.float32),
        jnp.zeros((heads_here, rows, HD), jnp.float32),
    )
    piece = lax.all_gather(own_pairs, "ep", axis=0, tiled=True)
    length = piece.shape[0]
    stride = min(length, rows * max(1, 512 // rows))
    while length % stride:
        stride = stride - 1

    def one_block(index, state):
        top, total, numer = state
        block = lax.dynamic_slice_in_dim(piece, index * stride, stride, 0)
        key_clip = clip_index(clip_lengths, index * stride + jnp.arange(stride, dtype=jnp.int32))
        scores = (
            jnp.einsum(
                "rhd,nd->hrn", query_heads, block[:, :HD], preferred_element_type=jnp.float32
            )
            * scale
        )
        same = (query_clip[:, None] == key_clip[None, :])[None, :, :]
        new_top = jnp.maximum(top, jnp.max(jnp.where(same, scores, -1e30), axis=2))
        weights = jnp.where(same, jnp.exp(scores - new_top[:, :, None]), 0.0)
        factor = jnp.exp(top - new_top)
        total = total * factor + jnp.sum(weights, axis=2)
        numer = numer * factor[:, :, None] + jnp.einsum(
            "hrn,nd->hrd",
            weights.astype(jnp.bfloat16),
            block[:, HD:],
            preferred_element_type=jnp.float32,
        )
        return (new_top, total, numer)

    top, total, numer = lax.fori_loop(0, length // stride, one_block, start_state)
    attended = (numer / total[:, :, None]).astype(jnp.bfloat16)
    half = residual.shape[1]
    out_heads = w_out.reshape(heads_here, HD, pool_size * half)
    moe_rows = residual.shape[0]
    start = jnp.int32(0)
    pieces = []
    for offset in range(lax.axis_size(("pool", "tp")) * moe_rows // rows):
        part = start // rows + offset
        weights = lax.dynamic_slice_in_dim(out_heads, part * half, half, 2)
        pieces.append(
            jnp.einsum("hrd,hde->re", attended, weights, preferred_element_type=jnp.float32)
        )
    mixed = lax.psum_scatter(
        jnp.concatenate(pieces, axis=0).astype(jnp.bfloat16),
        ("pool", "tp"),
        scatter_dimension=0,
        tiled=True,
    ).astype(jnp.float32)
    hidden_state = residual.astype(jnp.float32) + mixed
    squares = lax.psum(jnp.sum(hidden_state * hidden_state, axis=1), "pool")
    normed = (hidden_state * lax.rsqrt(squares / D + 1e-06)[:, None] * norm_gain[None, :]).astype(
        jnp.bfloat16
    )
    top_k = expert_ids.shape[1]
    local_experts = w_gate_up.shape[0]
    experts = local_experts * context_size * tensor_size
    capacity = 2 * moe_rows * top_k // experts
    flat = expert_ids.reshape(-1)
    marks = (flat[:, None] == jnp.arange(experts, dtype=jnp.int32)[None, :]).astype(jnp.int32)
    rank = jnp.sum(jnp.cumsum(marks, axis=0) * marks, axis=1) - 1
    slot = flat * capacity + rank
    source = jnp.arange(moe_rows * top_k, dtype=jnp.int32) // top_k
    outgoing = jnp.zeros((experts * capacity, half), jnp.bfloat16).at[slot].set(normed[source])
    hidden_width = w_down.shape[1]
    shaped = outgoing.reshape(experts, capacity, half)
    arrived = lax.all_to_all(shaped, ("ep", "tp"), split_axis=0, concat_axis=0, tiled=True)
    width = arrived.shape[1]
    grouped = arrived.reshape(-1, local_experts, width, half)
    both = jnp.einsum("slcd,ldf->slcf", grouped, w_gate_up, preferred_element_type=jnp.float32)
    both = lax.psum(both.astype(jnp.bfloat16), "pool").astype(jnp.float32)
    hidden = (jax.nn.silu(both[..., :hidden_width]) * both[..., hidden_width:]).astype(jnp.bfloat16)
    result = jnp.einsum(
        "slcf,lfd->slcd", hidden, w_down, preferred_element_type=jnp.float32
    ).astype(jnp.bfloat16)
    finished = result.reshape(-1, width, half)
    back = lax.all_to_all(finished, ("ep", "tp"), split_axis=0, concat_axis=0, tiled=True)
    back_rows = back.reshape(experts * capacity, half)[slot]
    gathered = back_rows.reshape(moe_rows, top_k, half).astype(jnp.float32)
    blended = jnp.sum(gathered * mix_weights[:, :, None], axis=1)
    return (hidden_state + blended).astype(jnp.bfloat16)


def solution(mesh):
    placed = (
        P(("grp", "ep"), ("pool", "tp")),
        P(("grp", "ep"), "pool"),
        P(("grp", "ep", "tp"), "pool"),
        P("pool"),
        P(("pool", "tp"), None),
        P(("ep", "tp"), "pool", None),
        P(("ep", "tp"), None, "pool"),
        P(("grp", "ep", "tp"), None),
        P(("grp", "ep", "tp"), None),
        P("grp"),
    )
    return jax.shard_map(
        body, mesh=mesh, in_specs=placed, out_specs=P(("grp", "ep", "tp"), "pool"), check_vma=False
    )
```
